256 devices in a mesh: look: 32 (over y_lo, z, core), swath: 8 (over y_hi, x).
Axes of the slice: x: 4, y: 4 (y_hi: 2, y_lo: 2; y = y_hi * 2 + y_lo), z: 8, core: 2. Of those that a mesh axis runs over, the one named last changes fastest.
Arguments:
- images: bfloat16 [64, 32, 2, 512, 512], P('look', 'swath'), may hold values from -6 to 6
- patch_weight: float32 [32], P('swath'), may hold values from 1 to 10
- pair_mask: int32 [64, 4], P('look'), may hold values 0 or 1
Outputs:
- drift: float32 [64, 4, 256, 256], P('look', None, 'swath')
The draws below stay inside these ranges and needn't reach their ends.
All inputs are finite; a program needn't handle non-finite values. No bound on the sum of `pair_mask` on one device may be relied on, other than what follows from the above.
Results may differ from the reference program's by a relative error of at most 0.015.
Values may be sent and summed in bfloat16 or wider, within the bound.
No kernel may reach another device: no remote copies, remote signals or barrier semaphores. Data moves between devices by JAX's collectives and lax.ppermute only.
A program may use at most 128 MiB of HBM per device.

```python
import math
import jax
import jax.numpy as jnp
from jax import lax

PIX = 512
BAND = 256
WIN = 256
LAGS = 4
LOOKS = 64
PATCHES = 32


def place_ends(drawn, own_key, smallest, largest):
    longest = drawn.shape.index(max(drawn.shape))
    spots = []
    for shift in (0, 1):
        where = [jax.random.randint(jax.random.fold_in(own_key, axis), (), 0, length) for axis, length in enumerate(drawn.shape)]
        where[longest] = (where[longest] + shift) % drawn.shape[longest]
        spots.append(tuple(where))
    return drawn.at[spots[0]].set(smallest).at[spots[1]].set(largest)


def level_of(own_key, extent, cuts, least, high):
    loudness, own = 1.0, jax.random.fold_in(own_key, 6)
    for axis_at, shards_of in cuts:
        steps = jnp.exp(jax.random.uniform(jax.random.fold_in(own, axis_at), (shards_of,), jnp.float32, least / len(cuts), high / len(cuts)))
        loudness = loudness * jnp.repeat(steps, extent[axis_at] // shards_of).reshape([-1 if axis == axis_at else 1 for axis in range(len(extent))])
    return loudness


def centred(key, shape, spread, limit, pieces=(), kind=jnp.bfloat16):
    factor_of = level_of(key, shape, pieces, -0.22, 0.18) if pieces else 1.0
    drawn = jax.random.normal(key, shape, jnp.float32) * spread * factor_of
    return jnp.minimum(jnp.maximum(drawn, -limit), limit).astype(kind)


def setup_inputs(seed: int = 0) -> dict:
    key_list = jax.random.split(jax.random.key(seed), 4)
    images = centred(key_list[0], (LOOKS, PATCHES, 2, PIX, PIX), 1.0, 6.0, ((0, 32), (1, 8)))
    patch_weight = jnp.clip(jnp.exp(math.log(10.0) - 2.3025851 * jax.random.uniform(key_list[1], (PATCHES,), jnp.float32) ** level_of(key_list[1], (PATCHES,), ((0, 8),), -0.2, 0.2)), 1.0, 10.0)
    pair_mask = place_ends((jax.random.randint(key_list[2], (LOOKS, LAGS), 0, 4) < 3).astype(jnp.int32), jax.random.fold_in(key_list[2], 1), 0, 1)
    return dict(images=images, patch_weight=patch_weight, pair_mask=pair_mask)


def tables(rows, cols, row_shift, col_shift, sign):
    row_ids = jnp.arange(rows, dtype=jnp.int32) - row_shift
    col_ids = jnp.arange(cols, dtype=jnp.int32) - col_shift
    phase = row_ids[:, None] * col_ids[None, :] % PIX
    angle = 2.0 * math.pi / PIX * phase.astype(jnp.float32)
    return (jnp.cos(angle).astype(jnp.bfloat16), (sign * jnp.sin(angle)).astype(jnp.bfloat16))

def fdot(form, left, right):
    return jnp.einsum(form, left.astype(jnp.float32), right.astype(jnp.float32))

def spectra(block, fwd_re, fwd_im):
    img_re = block[:, 0]
    img_im = block[:, 1]
    rows_re = (fdot('kn,anm->akm', fwd_re, img_re) - fdot('kn,anm->akm', fwd_im, img_im)).astype(jnp.bfloat16)
    rows_im = (fdot('kn,anm->akm', fwd_re, img_im) + fdot('kn,anm->akm', fwd_im, img_re)).astype(jnp.bfloat16)
    spec_re = (fdot('akm,lm->akl', rows_re, fwd_re) - fdot('akm,lm->akl', rows_im, fwd_im)).astype(jnp.bfloat16)
    spec_im = (fdot('akm,lm->akl', rows_re, fwd_im) + fdot('akm,lm->akl', rows_im, fwd_re)).astype(jnp.bfloat16)
    return jnp.stack([spec_re, spec_im], axis=1)

def surface_of(own, partner, weights, inv_re, inv_im):
    own_re = own[:, 0].astype(jnp.float32)
    own_im = own[:, 1].astype(jnp.float32)
    par_re = partner[:, 0].astype(jnp.float32)
    par_im = partner[:, 1].astype(jnp.float32)
    cross_re = (own_re * par_re + own_im * par_im).astype(jnp.bfloat16)
    cross_im = (own_im * par_re - own_re * par_im).astype(jnp.bfloat16)
    shift_re = (fdot('tf,pfg->ptg', inv_re, cross_re) - fdot('tf,pfg->ptg', inv_im, cross_im)).astype(jnp.bfloat16)
    shift_im = (fdot('tf,pfg->ptg', inv_re, cross_im) + fdot('tf,pfg->ptg', inv_im, cross_re)).astype(jnp.bfloat16)
    real_part = fdot('ptg,ug->ptu', shift_re, inv_re) - fdot('ptg,ug->ptu', shift_im, inv_im)
    return jnp.einsum('p,ptu->tu', weights, real_part)

def reference(images, patch_weight, pair_mask):
    fwd_re, fwd_im = tables(BAND, PIX, BAND // 2, 0, -1.0)
    inv_re, inv_im = tables(WIN, BAND, WIN // 2, BAND // 2, 1.0)
    spectrum = lax.map(lambda block: spectra(block, fwd_re, fwd_im), images)

    def energy_of(spec):
        sq = spec.astype(jnp.float32)
        return jnp.sum(patch_weight * lax.optimization_barrier(jnp.sum(sq * sq, axis=(1, 2, 3))))
    energy = lax.map(energy_of, spectrum)
    scale = BAND * math.sqrt(PATCHES)

    def one_look(look):
        own = lax.dynamic_index_in_dim(spectrum, look, 0, keepdims=False)
        outs = []
        for offset in (1, 2, 3, LOOKS // 2):
            mate = ((look + offset) % LOOKS).astype(jnp.int32)
            partner = lax.dynamic_index_in_dim(spectrum, mate, 0, keepdims=False)
            surf = surface_of(own, partner, patch_weight, inv_re, inv_im)
            denom = jnp.sqrt(energy[look] * energy[mate])
            outs.append(surf * scale / denom)
        return jnp.stack(outs, axis=0)
    surfaces = lax.map(one_look, jnp.arange(LOOKS, dtype=jnp.int32))
    return surfaces * pair_mask.astype(jnp.float32)[:, :, None, None]
```

```python
import functools
import math

import jax
import jax.numpy as jnp
import numpy as np
from jax import lax
from jax.experimental import pallas as pl
from jax.experimental.pallas import tpu as pltpu
from jax.sharding import PartitionSpec as P

PIX = 512
BAND = 256
WIN = 256
HALF = 256
CHUNK = 2
EROWS = 16
BF = jnp.bfloat16
F32 = jnp.float32


def phases(rows, cols):
    phase = (rows[:, None] * cols[None, :]) % PIX
    angle = (2.0 * math.pi / PIX * phase.astype(np.float32)).astype(np.float32)
    return np.cos(angle), np.sin(angle)


def make_tables():
    order = np.concatenate([np.arange(0, BAND, 2), np.arange(1, BAND, 2)])
    n0 = np.arange(HALF)
    right, left = [], []
    for parity in range(2):
        ks = np.arange(parity, BAND, 2) - BAND // 2
        re, im = phases(ks, n0)
        im = -im
        right.append(np.block([[re.T, im.T], [-im.T, re.T]]))
        left.append(np.block([[re, -im], [im, re]]))
    ts = np.arange(WIN) - WIN // 2
    gre, gim = phases(ts, order - BAND // 2)
    first = np.block([[gre, -gim], [gim, gre]])
    second = np.concatenate([gre.T, -gim.T], axis=0)
    cast = lambda a: jnp.asarray(np.asarray(a, np.float32).astype(jnp.bfloat16))
    return cast(np.stack(right)), cast(np.stack(left)), cast(first), cast(second)


def dot(a, b):
    return jnp.dot(a, b, preferred_element_type=F32)


def forward_kernel(first_patch, flags, img, right, left, e0, e1, osend, wrapped, xbuf, sems):
    steps = [(p, k) for p in range(CHUNK) for k in range(2)]
    copies = [
        pltpu.make_async_copy(img.at[k, first_patch + p], xbuf.at[i], sems.at[i])
        for i, (p, k) in enumerate(steps)
    ]
    for c in copies:
        c.start()
    lo = flags[0]
    zero = flags[1]
    for i, (p, k) in enumerate(steps):
        copies[i].wait()
        halves = {}
        for part in range(2):
            x = xbuf.at[i, part]
            x00 = x[:HALF, :HALF].astype(F32)
            x01 = x[:HALF, HALF:].astype(F32)
            x10 = x[HALF:, :HALF].astype(F32)
            x11 = x[HALF:, HALF:].astype(F32)
            a, b = x00 + x10, x01 + x11
            c, d = x00 - x10, x01 - x11
            halves[part] = ((a + b).astype(BF), (a - b).astype(BF), (c + d).astype(BF), (c - d).astype(BF))
        y = {}
        for lp in range(2):
            for kp in range(2):
                both = jnp.concatenate([halves[0][2 * kp + lp], halves[1][2 * kp + lp]], axis=1)
                y[kp, lp] = dot(both, right[lp]).astype(BF)
        for kp in range(2):
            stacked = jnp.concatenate(
                [
                    jnp.concatenate([y[kp, 0][:, :128], y[kp, 1][:, :128]], axis=1),
                    jnp.concatenate([y[kp, 0][:, 128:], y[kp, 1][:, 128:]], axis=1),
                ],
                axis=0,
            )
            spec = dot(left[kp], stacked).astype(BF)
            rows = slice(128 * kp, 128 * kp + 128)
            own = e1 if k else e0
            for part in range(2):
                own[p, part, rows, :] = spec[128 * part : 128 * part + 128]

            @pl.when(lo == 1 - k)
            def _():
                for part in range(2):
                    osend[p, part, rows, :] = spec[128 * part : 128 * part + 128]

            @pl.when(zero == 1 - k)
            def _():
                for part in range(2):
                    wrapped[p, part, rows, :] = spec[128 * part : 128 * part + 128]


def forward(first_patch, flags, images, right, left):
    shape = jax.ShapeDtypeStruct((CHUNK, 2, BAND, BAND), BF)
    vm = pl.BlockSpec(memory_space=pltpu.VMEM)
    return pl.pallas_call(
        functools.partial(forward_kernel, first_patch),
        out_shape=[shape] * 4,
        in_specs=[pl.BlockSpec(memory_space=pltpu.SMEM), pl.BlockSpec(memory_space=pl.ANY), vm, vm],
        out_specs=[vm] * 4,
        scratch_shapes=[
            pltpu.VMEM((2 * CHUNK, 2, PIX, PIX), BF),
            pltpu.SemaphoreType.DMA((2 * CHUNK,)),
        ],
        compiler_params=pltpu.CompilerParams(vmem_limit_bytes=28 * 2**20),
        cost_estimate=pl.CostEstimate(
            flops=2 * CHUNK * 2 * 201 * 10**6, bytes_accessed=CHUNK * 2 * 2**20, transcendentals=0
        ),
        name="forward",
    )(flags, images, right, left)


PAIRS = 7


def cross_block(first_patch, flags, weight, refs, row, lane, acc, energy):
    e0, e1, pl0, pl1, q1, op = refs
    lo = flags[0] > 0
    swapped = flags[2] > 0

    def load(ref, p):
        return [ref[p, part, pl.ds(row, 16), lane].astype(F32) for part in range(2)]

    def pick(cond, a, b):
        return [jnp.where(cond, u, v) for u, v in zip(a, b)]

    for p in range(CHUNK):
        w = weight[first_patch + p]
        own0, own1 = load(e0, p), load(e1, p)
        a, b = load(pl0, p), load(pl1, p)
        next0, next1 = pick(swapped, b, a), pick(swapped, a, b)
        prev, opp = load(q1, p), load(op, p)
        for i, s in enumerate([own0, own1, next0, next1, prev, opp]):
            energy[i] = energy[i] + w * (s[0] * s[0] + s[1] * s[1])
        w0 = [w * v for v in own0]
        wq = [w * v for v in prev]
        wo = [w * v for v in pick(lo, own1, own0)]
        pairs = [(w0, own1), (w0, next0), (w0, next1), (wq, own0), (wq, own1), (wq, next0), (wo, opp)]
        for i, (l, m) in enumerate(pairs):
            acc[2 * i] = acc[2 * i] + (l[0] * m[0] + l[1] * m[1])
            acc[2 * i + 1] = acc[2 * i + 1] + (l[1] * m[0] - l[0] * m[1])


def cross_kernel(first_patch, flags, weight, e0, e1, pl0, pl1, q1, op, acc_out, energy_out):
    refs = (e0, e1, pl0, pl1, q1, op)
    energy_out[...] = jnp.zeros_like(energy_out)

    @pl.loop(0, BAND // 16)
    def _(block):
        row = pl.multiple_of(block * 16, 16)
        for half in range(2):
            lane = slice(128 * half, 128 * half + 128)
            acc = [jnp.zeros((16, 128), F32)] * (2 * PAIRS)
            energy = [jnp.zeros((16, 128), F32)] * 6
            cross_block(first_patch, flags, weight, refs, row, lane, acc, energy)
            for i in range(2 * PAIRS):
                acc_out[i, pl.ds(row, 16), lane] = acc[i]
            for i in range(6):
                energy_out[i] += energy[i][:8] + energy[i][8:]


def cross_first(flags, weight, pieces):
    vm = pl.BlockSpec(memory_space=pltpu.VMEM)
    sm = pl.BlockSpec(memory_space=pltpu.SMEM)
    return pl.pallas_call(
        functools.partial(cross_kernel, 0),
        out_shape=[
            jax.ShapeDtypeStruct((2 * PAIRS, BAND, BAND), F32),
            jax.ShapeDtypeStruct((6, 8, 128), F32),
        ],
        in_specs=[sm, sm] + [vm] * 6,
        out_specs=[vm, vm],
        compiler_params=pltpu.CompilerParams(vmem_limit_bytes=24 * 2**20),
        cost_estimate=pl.CostEstimate(flops=20 * 10**6, bytes_accessed=6 * 2**20, transcendentals=0),
        name="cross",
    )(flags, weight, *pieces)


def split(value):
    hi = value.astype(BF).astype(F32)
    lo = (value - hi).astype(BF).astype(F32)
    return hi, lo


def energy_rows(values):
    his, los = zip(*[split(v) for v in values])
    pad = [jnp.zeros_like(values[0])] * (EROWS - 12)
    return jnp.concatenate(list(his) + list(los) + pad, axis=0).astype(BF)


def surface_kernel(
    first_patch, flags, weight, e0, e1, pl0, pl1, q1, op, acc_in, energy_in, first, second, s0, s1, s2, s3,
    cross, surf, energy_sum,
):
    refs = (e0, e1, pl0, pl1, q1, op)
    energy_sum[...] = energy_in[...]

    @pl.loop(0, BAND // 16)
    def _(block):
        row = pl.multiple_of(block * 16, 16)
        rowi = pl.multiple_of(block * 16 + BAND, 16)
        for half in range(2):
            lane = slice(128 * half, 128 * half + 128)
            acc = [acc_in[i, pl.ds(row, 16), lane] for i in range(2 * PAIRS)]
            energy = [jnp.zeros((16, 128), F32)] * 6
            cross_block(first_patch, flags, weight, refs, row, lane, acc, energy)
            for i in range(PAIRS):
                cross[i, pl.ds(row, 16), lane] = acc[2 * i].astype(BF)
                cross[i, pl.ds(rowi, 16), lane] = acc[2 * i + 1].astype(BF)
            cross[PAIRS, pl.ds(row, 16), lane] = acc[2 * PAIRS - 2].astype(BF)
            cross[PAIRS, pl.ds(rowi, 16), lane] = (-acc[2 * PAIRS - 1]).astype(BF)
            for i in range(6):
                energy_sum[i] += energy[i][:8] + energy[i][8:]

    for i in range(PAIRS + 1):
        shifted = dot(first[...], cross[i]).astype(BF)
        surf[i] = (dot(shifted[:WIN], second[:BAND]) + dot(shifted[WIN:], second[BAND:])).astype(BF)

    totals = []
    for i in range(6):
        total = jnp.sum(jnp.sum(energy_sum[i], axis=1, keepdims=True), axis=0, keepdims=True)
        totals.append(jnp.broadcast_to(total, (1, WIN)))
    erows = energy_rows(totals)
    x = flags[3]
    for slot, out in enumerate((s0, s1, s2, s3)):
        dest = lax.rem(x + slot, 4)
        for yh in range(2):
            start = pl.multiple_of((4 * yh + dest) * 32, 32)
            for i in range(PAIRS + 1):
                out[yh, 32 * i : 32 * i + 32, :] = surf[i, pl.ds(start, 32), :]
            out[yh, 32 * (PAIRS + 1) :, :] = erows


ROWS = 32 * (PAIRS + 1) + EROWS


def surfaces(flags, weight, pieces, acc, energy, first, second):
    vm = pl.BlockSpec(memory_space=pltpu.VMEM)
    sm = pl.BlockSpec(memory_space=pltpu.SMEM)
    return pl.pallas_call(
        functools.partial(surface_kernel, CHUNK),
        out_shape=[jax.ShapeDtypeStruct((2, ROWS, WIN), BF)] * 4,
        in_specs=[sm, sm] + [vm] * 10,
        out_specs=[vm] * 4,
        scratch_shapes=[
            pltpu.VMEM((PAIRS + 1, 2 * BAND, BAND), BF),
            pltpu.VMEM((PAIRS + 1, WIN, WIN), BF),
            pltpu.VMEM((6, 8, 128), F32),
        ],
        compiler_params=pltpu.CompilerParams(vmem_limit_bytes=28 * 2**20),
        cost_estimate=pl.CostEstimate(flops=1600 * 10**6, bytes_accessed=8 * 2**20, transcendentals=0),
        name="surfaces",
    )(flags, weight, *pieces, acc, energy, first, second)


def sum_energy(block):
    return [block[i : i + 1] + block[6 + i : 7 + i] for i in range(6)]


def gather_kernel(flags, a, b, c, d, keep, near_other, back_same, back_other, opp_same, opp_other):
    yh = flags[4]
    base = 32 * (PAIRS + 1)
    for which, (near_out, back_out, opp_out) in enumerate(
        ((keep, back_same, opp_same), (near_other, back_other, opp_other))
    ):
        h = yh if which == 0 else 1 - yh
        blocks = [r[h].astype(F32) for r in (a, b, c, d)]
        total = (blocks[0] + blocks[1]) + (blocks[2] + blocks[3])
        values = sum_energy(total[base:])
        erows = energy_rows(values)
        near_out[0:96] = total[0:96].astype(near_out.dtype)
        near_out[96:128] = total[192:224].astype(near_out.dtype)
        near_out[128:] = erows.astype(near_out.dtype)
        back_out[0:96] = total[96:192].astype(BF)
        back_out[96:] = erows
        opp_out[0:32] = total[224:256].astype(BF)
        opp_out[32:] = erows


def gather(flags, parts):
    vm = pl.BlockSpec(memory_space=pltpu.VMEM)
    sm = pl.BlockSpec(memory_space=pltpu.SMEM)
    return pl.pallas_call(
        gather_kernel,
        out_shape=[
            jax.ShapeDtypeStruct((144, WIN), F32),
            jax.ShapeDtypeStruct((144, WIN), BF),
            jax.ShapeDtypeStruct((112, WIN), BF),
            jax.ShapeDtypeStruct((112, WIN), BF),
            jax.ShapeDtypeStruct((48, WIN), BF),
            jax.ShapeDtypeStruct((48, WIN), BF),
        ],
        in_specs=[sm] + [vm] * 4,
        out_specs=[vm] * 6,
        compiler_params=pltpu.CompilerParams(vmem_limit_bytes=16 * 2**20),
        cost_estimate=pl.CostEstimate(flops=10**6, bytes_accessed=2**20, transcendentals=0),
        name="gather",
    )(flags, *parts)


def final_kernel(scale, flags, mask, keep, near, back_a, back_b, opp_a, opp_b, out):
    lo = flags[0]
    mine = keep[...] + near[...].astype(F32)
    back = back_a[...].astype(F32) + back_b[...].astype(F32)
    other = opp_a[...].astype(F32) + opp_b[...].astype(F32)

    def factor(el, em):
        return scale / jnp.sqrt(el * em)

    ev = sum_energy(mine[128:])
    for j in range(3):
        f = factor(ev[0], ev[1 + j]) * mask[0, j].astype(F32)
        out[0, j] = mine[32 * j : 32 * j + 32] * f
    own_opp = mine[96:128] * factor(jnp.where(lo > 0, ev[1], ev[0]), ev[5])
    eb = sum_energy(back[96:])
    mates = (eb[0], eb[1], eb[2])
    for j in range(3):
        f = factor(eb[4], mates[j]) * mask[1, j].astype(F32)
        out[1, j] = back[32 * j : 32 * j + 32] * f
    eo = sum_energy(other[32:])
    other_opp = other[:32] * factor(jnp.where(lo > 0, eo[0], eo[1]), eo[5])
    out[0, 3] = jnp.where(lo > 0, other_opp, own_opp) * mask[0, 3].astype(F32)
    out[1, 3] = jnp.where(lo > 0, own_opp, other_opp) * mask[1, 3].astype(F32)


def final(scale, flags, mask, parts):
    vm = pl.BlockSpec(memory_space=pltpu.VMEM)
    sm = pl.BlockSpec(memory_space=pltpu.SMEM)
    return pl.pallas_call(
        functools.partial(final_kernel, scale),
        out_shape=jax.ShapeDtypeStruct((2, 4, 32, WIN), F32),
        in_specs=[sm, sm] + [vm] * 6,
        out_specs=vm,
        compiler_params=pltpu.CompilerParams(vmem_limit_bytes=16 * 2**20),
        cost_estimate=pl.CostEstimate(flops=10**6, bytes_accessed=2**20, transcendentals=0),
        name="final",
    )(flags, mask, *parts)


def per_device(images, patch_weight, pair_mask):
    nlook = lax.axis_size("look")
    nswath = lax.axis_size("swath")
    ring = nlook // 2
    look = lax.axis_index("look")
    swath = lax.axis_index("swath")
    lo = (look >= ring).astype(jnp.int32)
    is_zero = (look == 0).astype(jnp.int32)
    is_last = (look == nlook - 1).astype(jnp.int32)
    flags = jnp.stack([lo, is_zero, is_last, swath % 4, swath // 4, lo, lo, lo]).astype(jnp.int32)
    edge = look % ring == 0
    right, left, first, second = make_tables()

    def over_look(array, to):
        return lax.ppermute(array, "look", [(i, to(i)) for i in range(nlook)])

    def over_swath(array, by):
        return lax.ppermute(array, "swath", [(i, i // 4 * 4 + (i + by) % 4) for i in range(nswath)])

    def over_both(array, to_look, flip):
        perm = [
            (i * nswath + s, to_look(i) * nswath + ((s + nswath // 2) % nswath if flip else s))
            for i in range(nlook)
            for s in range(nswath)
        ]
        return lax.ppermute(array, ("look", "swath"), perm)

    behind = lambda i: (i - 1) % nlook
    across = lambda i: (i + ring) % nlook
    turn = lambda i: i // ring * ring + (i - 1) % ring
    pieces = []
    for c in range(2):
        e0, e1, osend, wrapped = forward(CHUNK * c, flags, images, right, left)
        op = over_look(osend, across)
        pl1 = over_look(wrapped, behind)
        q1 = over_look(e1, lambda i: (i + 1) % nlook)
        pl0 = over_look(jnp.where(edge, op, e0), turn)
        pieces.append((e0, e1, pl0, pl1, q1, op))
    acc, energy = cross_first(flags, patch_weight, pieces[0])
    s0, s1, s2, s3 = surfaces(flags, patch_weight, pieces[1], acc, energy, first, second)
    r1 = over_swath(s1, 1)
    r2 = over_swath(s2, 2)
    r3 = over_swath(s3, 3)
    keep, near, back_same, back_other, opp_same, opp_other = gather(flags, (s0, r1, r2, r3))
    got = (
        over_both(near, lambda i: i, True),
        over_both(back_same, behind, False),
        over_both(back_other, behind, True),
        over_both(opp_same, across, False),
        over_both(opp_other, across, True),
    )
    scale = BAND * math.sqrt(patch_weight.shape[0] * nswath)
    return final(scale, flags, pair_mask, (keep,) + got)


def solution(mesh):
    return jax.shard_map(
        per_device,
        mesh=mesh,
        in_specs=(P("look", "swath", None, None, None), P("swath"), P("look", None)),
        out_specs=P("look", None, "swath", None),
        check_vma=False,
    )
```

```python
import functools
import math

import jax
import jax.numpy as jnp
import numpy as np
from jax import lax
from jax.experimental import pallas as pl
from jax.experimental.pallas import tpu as pltpu
from jax.sharding import PartitionSpec as P

PIX = 512
BAND = 256
WIN = 256
HALF = 256
CHUNK = 2
EROWS = 16
TABLES = 32
REST_LIMIT = 52
BF = jnp.bfloat16
F32 = jnp.float32


def phases(rows, cols):
    phase = (rows[:, None] * cols[None, :]) % PIX
    angle = (2.0 * math.pi / PIX * phase.astype(np.float32)).astype(np.float32)
    return np.cos(angle), np.sin(angle)


def make_tables():
    order = np.concatenate([np.arange(0, BAND, 2), np.arange(1, BAND, 2)])
    n0 = np.arange(HALF)
    left = []
    for parity in range(2):
        ks = np.arange(parity, BAND, 2) - BAND // 2
        re, im = phases(ks, n0)
        im = -im
        left.append(np.block([[re, -im], [im, re]]))
    ts = np.arange(WIN) - WIN // 2
    gre, gim = phases(ts, order - BAND // 2)
    first = np.block([[gre, -gim], [gim, gre]])
    second = np.concatenate([gre, -gim], axis=1)
    cast = lambda a: jnp.asarray(np.asarray(a, np.float32).astype(jnp.bfloat16))
    room = np.zeros((TABLES - 2, 256, 512))
    return cast(np.concatenate([np.stack(left), room])), cast(np.stack([first[:256], first[256:], second]))


def place():
    look = lax.axis_index("look")
    swath = lax.axis_index("swath")
    nlook = lax.axis_size("look")
    return dict(
        lo=(look >= nlook // 2).astype(jnp.int32),
        zero=look == 0,
        last=look == nlook - 1,
        x=lax.rem(swath, 4),
        yh=swath // 4,
    )


def dot(a, b):
    return jnp.dot(a, b, preferred_element_type=F32)


def dot_nt(a, b):
    return lax.dot_general(a, b, (((1,), (1,)), ((), ())), preferred_element_type=F32)


def butterflies(x):
    x00 = x[:HALF, :HALF].astype(F32)
    x01 = x[:HALF, HALF:].astype(F32)
    x10 = x[HALF:, :HALF].astype(F32)
    x11 = x[HALF:, HALF:].astype(F32)
    a, b = x00 + x10, x01 + x11
    c, d = x00 - x10, x01 - x11
    return [v.astype(BF) for v in (a + b, a - b, c + d, c - d)]


def image_pair(xbuf, at, tab, hbuf, ybuf, store):
    for k in range(2):
        for part in range(2):
            for q, h in enumerate(butterflies(xbuf.at[at + k, part])):
                kp, lp = q // 2, q % 2
                row = 512 * k + 256 * kp
                hbuf[lp, row : row + 256, 256 * part : 256 * part + 256] = h
    for lp in range(2):
        y = dot_nt(hbuf[lp], tab[lp]).astype(BF)
        for k in range(2):
            for kp in range(2):
                block = y[512 * k + 256 * kp : 512 * k + 256 * kp + 256]
                lane = 256 * k + 128 * lp
                ybuf[kp, :256, lane : lane + 128] = block[:, :128]
                ybuf[kp, 256:, lane : lane + 128] = block[:, 128:]
    for kp in range(2):
        spec = dot(tab[kp], ybuf[kp]).astype(BF)
        for k in range(2):
            for part in range(2):
                store(k, part, kp, spec[128 * part : 128 * part + 128, 256 * k : 256 * k + 256])


def image_copies(img, look, patches, xbuf, sems):
    return [
        pltpu.make_async_copy(img.at[look, p], xbuf.at[i], sems.at[i]) for i, p in enumerate(patches)
    ]


def send_kernel(patches, img, tables, out, xbuf, tab, hbuf, ybuf, sems):
    copies = image_copies(img, 1 - place()["lo"], patches, xbuf, sems)
    load = pltpu.make_async_copy(tables.at[pl.ds(0, 2)], tab, sems.at[len(patches)])
    for c in copies[:1] + [load] + copies[1:]:
        c.start()
    for c in copies + [load]:
        c.wait()

    def store(k, part, kp, value):
        out[k, part, 128 * kp : 128 * kp + 128, :] = value

    image_pair(xbuf, 0, tab, hbuf, ybuf, store)


def rest_kernel(
    img, tables, sent_a, sent_b, e0_a, e0_b, e1_a, e1_b, wrapped_a, wrapped_b, xbuf, tab, hbuf, ybuf, sems
):
    at = place()
    copies = image_copies(img, 1 - at["lo"], (2, 3), xbuf, sems)
    copies += image_copies(img, at["lo"], range(4), xbuf.at[pl.ds(2, 4)], sems.at[pl.ds(2, 4)])
    load = pltpu.make_async_copy(tables.at[pl.ds(0, 2)], tab, sems.at[6])
    for c in copies[:1] + [load] + copies[1:]:
        c.start()
    lo = at["lo"] > 0
    zero = at["zero"]
    load.wait()

    def keep(k, part, kp, value):
        sent_b[k, part, 128 * kp : 128 * kp + 128, :] = value

    for pair in range(3):
        for c in copies[2 * pair : 2 * pair + 2]:
            c.wait()

        def store(k, part, kp, value):
            rows = slice(128 * kp, 128 * kp + 128)
            sent, e0, e1, wrapped = ((sent_a, e0_a, e1_a, wrapped_a), (sent_b, e0_b, e1_b, wrapped_b))[pair - 1]
            other = sent[k, part, rows, :]
            v0 = jnp.where(lo, other, value)
            v1 = jnp.where(lo, value, other)
            e0[k, part, rows, :] = v0
            e1[k, part, rows, :] = v1
            wrapped[k, part, rows, :] = jnp.where(zero, v0, v1)

        image_pair(xbuf, 2 * pair, tab, hbuf.at[pair], ybuf.at[pair], store if pair else keep)


VM = pl.BlockSpec(memory_space=pltpu.VMEM)
SM = pl.BlockSpec(memory_space=pltpu.SMEM)
ANY = pl.BlockSpec(memory_space=pl.ANY)


def call(kernel, outs, ins, scratch, limit, flops, name):
    specs = []
    for kind, _ in ins:
        specs.append({"s": SM, "v": VM, "a": ANY}[kind])
    return pl.pallas_call(
        kernel,
        out_shape=[jax.ShapeDtypeStruct(s, t) for s, t in outs],
        in_specs=specs,
        out_specs=[VM] * len(outs),
        scratch_shapes=scratch,
        compiler_params=pltpu.CompilerParams(vmem_limit_bytes=limit * 2**20),
        cost_estimate=pl.CostEstimate(flops=flops * 10**6, bytes_accessed=2**20, transcendentals=0),
        name=name,
    )(*[a for _, a in ins])


def forward_send(patches, images, tables):
    return call(
        functools.partial(send_kernel, patches),
        [((2, 2, BAND, BAND), BF)],
        [("a", images), ("a", tables)],
        [
            pltpu.VMEM((2, 2, PIX, PIX), BF),
            pltpu.VMEM((2, 256, 512), BF),
            pltpu.VMEM((2, 1024, 512), BF),
            pltpu.VMEM((2, 512, 512), BF),
            pltpu.SemaphoreType.DMA((3,)),
        ],
        57,
        1200,
        "forward_send",
    )[0]


def forward_rest(images, tables, sent_a):
    return call(
        rest_kernel,
        [((2, 2, BAND, BAND), BF)] * 7,
        [("a", images), ("a", tables), ("v", sent_a)],
        [
            pltpu.VMEM((6, 2, PIX, PIX), BF),
            pltpu.VMEM((2, 256, 512), BF),
            pltpu.VMEM((3, 2, 1024, 512), BF),
            pltpu.VMEM((3, 2, 512, 512), BF),
            pltpu.SemaphoreType.DMA((7,)),
        ],
        REST_LIMIT,
        3600,
        "forward_rest",
    )


def load_block(ref, p, row, lane):
    return [ref[p, part, pl.ds(row, 16), lane].astype(F32) for part in range(2)]


def accumulate(acc, i, l, m):
    acc[2 * i] = acc[2 * i] + (l[0] * m[0] + l[1] * m[1])
    acc[2 * i + 1] = acc[2 * i + 1] + (l[1] * m[0] - l[0] * m[1])


def add_energy(energy, i, w, s):
    energy[i] = energy[i] + w * (s[0] * s[0] + s[1] * s[1])


def pick(cond, a, b):
    return [jnp.where(cond, u, v) for u, v in zip(a, b)]


def inverse(tab, cross, surf, pairs):
    for i in range(pairs):
        shifted = dot(tab[0], cross[i]).astype(BF)
        low = dot(tab[1], cross[i]).astype(BF)
        surf[i] = (dot_nt(shifted, tab[2, :, :BAND]) + dot_nt(low, tab[2, :, BAND:])).astype(BF)


def emit(surf, pairs, outs, erows):
    x = place()["x"]
    for slot, out in enumerate(outs):
        dest = lax.rem(x + slot, 4)
        for yh in range(2):
            start = pl.multiple_of((4 * yh + dest) * 32, 32)
            for i in range(pairs):
                out[yh, 32 * i : 32 * i + 32, :] = surf[i, pl.ds(start, 32), :]
            out[yh, 32 * pairs :, :] = erows


def split(value):
    hi = value.astype(BF).astype(F32)
    return hi, (value - hi).astype(BF).astype(F32)


def energy_rows(values):
    his, los = zip(*[split(v) for v in values])
    pad = [jnp.zeros_like(values[0])] * (EROWS - 2 * len(values))
    return jnp.concatenate(list(his) + list(los) + pad, axis=0).astype(BF)


def total_rows(energy_sum, count):
    totals = []
    for i in range(count):
        total = jnp.sum(jnp.sum(energy_sum[i], axis=1, keepdims=True), axis=0, keepdims=True)
        totals.append(jnp.broadcast_to(total, (1, WIN)))
    return energy_rows(totals)


def blocks(body):
    @pl.loop(0, BAND // 16)
    def _(block):
        row = pl.multiple_of(block * 16, 16)
        rowi = pl.multiple_of(block * 16 + BAND, 16)
        for half in range(2):
            body(row, rowi, slice(128 * half, 128 * half + 128))


def zeros(count):
    return [jnp.zeros((16, 128), F32)] * count


def early_kernel(
    weight, tab, e0_a, e0_b, e1_a, e1_b, op_a, op_b, s0, s1, s2, s3, energy_out, cross, surf
):
    lo = place()["lo"] > 0
    energy_out[...] = jnp.zeros_like(energy_out)

    def body(row, rowi, lane):
        acc, energy = zeros(4), zeros(3)
        for p in range(4):
            w = weight[p]
            own0 = load_block((e0_a, e0_b)[p // 2], p % 2, row, lane)
            own1 = load_block((e1_a, e1_b)[p // 2], p % 2, row, lane)
            opp = load_block((op_a, op_b)[p // 2], p % 2, row, lane)
            for i, v in enumerate((own0, own1, opp)):
                add_energy(energy, i, w, v)
            accumulate(acc, 0, [w * v for v in own0], own1)
            accumulate(acc, 1, [w * v for v in pick(lo, own1, own0)], opp)
        for i in range(2):
            cross[i, pl.ds(row, 16), lane] = acc[2 * i].astype(BF)
            cross[i, pl.ds(rowi, 16), lane] = acc[2 * i + 1].astype(BF)
        cross[2, pl.ds(row, 16), lane] = acc[2].astype(BF)
        cross[2, pl.ds(rowi, 16), lane] = (-acc[3]).astype(BF)
        for i in range(3):
            energy_out[i] += energy[i][:8] + energy[i][8:]

    blocks(body)
    inverse(tab, cross, surf, 3)
    emit(surf, 3, (s0, s1, s2, s3), total_rows(energy_out, 3))


def late_kernel(
    weight, tab, energy_in, e0_a, e0_b, e1_a, e1_b, q1_a, q1_b, pl0_a, pl0_b, pl1_a, pl1_b,
    s0, s1, s2, s3, cross, surf, energy_sum,
):
    swapped = place()["last"]
    energy_sum[0:2] = energy_in[0:2]
    energy_sum[2:5] = jnp.zeros((3, 8, 128), F32)

    def body(row, rowi, lane):
        acc, energy = zeros(10), zeros(3)
        for p in range(4):
            w = weight[p]
            own0, own1, prev, a, b = [
                load_block(pair[p // 2], p % 2, row, lane)
                for pair in ((e0_a, e0_b), (e1_a, e1_b), (q1_a, q1_b), (pl0_a, pl0_b), (pl1_a, pl1_b))
            ]
            next0, next1 = pick(swapped, b, a), pick(swapped, a, b)
            for i, v in enumerate((prev, next0, next1)):
                add_energy(energy, i, w, v)
            w0 = [w * v for v in own0]
            wq = [w * v for v in prev]
            for i, (l, m) in enumerate(
                ((w0, next0), (w0, next1), (wq, own0), (wq, own1), (wq, next0))
            ):
                accumulate(acc, i, l, m)
        for i in range(5):
            cross[i, pl.ds(row, 16), lane] = acc[2 * i].astype(BF)
            cross[i, pl.ds(rowi, 16), lane] = acc[2 * i + 1].astype(BF)
        for i in range(3):
            energy_sum[2 + i] += energy[i][:8] + energy[i][8:]

    blocks(body)
    inverse(tab, cross, surf, 5)
    emit(surf, 5, (s0, s1, s2, s3), total_rows(energy_sum, 5))


def surfaces(kernel, pairs, ins, more, scratch, name):
    return call(
        kernel,
        [((2, 32 * pairs + EROWS, WIN), BF)] * 4 + more,
        ins,
        [pltpu.VMEM((pairs, 2 * BAND, BAND), BF), pltpu.VMEM((pairs, WIN, WIN), BF)] + scratch,
        24,
        250 * pairs,
        name,
    )


def sum_energy(block, count):
    return [block[i : i + 1] + block[count + i : count + i + 1] for i in range(count)]


def add_parts(parts, h):
    a, b, c, d = [r[h].astype(F32) for r in parts]
    return (a + b) + (c + d)


def gather_early_kernel(a, b, c, d, keep, near, opp_same, opp_other):
    yh = place()["yh"]
    for h, (near_out, opp_out) in ((yh, (keep, opp_same)), (1 - yh, (near, opp_other))):
        total = add_parts((a, b, c, d), h)
        erows = energy_rows(sum_energy(total[96:], 3))
        near_out[0:64] = total[0:64].astype(near_out.dtype)
        near_out[64:] = erows.astype(near_out.dtype)
        opp_out[0:32] = total[64:96].astype(BF)
        opp_out[32:] = erows


def gather_late_kernel(a, b, c, d, keep, near, back_same, back_other):
    yh = place()["yh"]
    for h, (near_out, back_out) in ((yh, (keep, back_same)), (1 - yh, (near, back_other))):
        total = add_parts((a, b, c, d), h)
        erows = energy_rows(sum_energy(total[160:], 5))
        near_out[0:64] = total[0:64].astype(near_out.dtype)
        near_out[64:] = erows.astype(near_out.dtype)
        back_out[0:96] = total[64:160].astype(BF)
        back_out[96:] = erows


def final_kernel(scale, mask, keep, near, opp_a, opp_b, keep2, near2, back_a, back_b, out):
    lo = place()["lo"] > 0
    mine = keep[...] + near[...].astype(F32)
    other = opp_a[...].astype(F32) + opp_b[...].astype(F32)
    mine2 = keep2[...] + near2[...].astype(F32)
    back = back_a[...].astype(F32) + back_b[...].astype(F32)

    def factor(el, em):
        return scale / jnp.sqrt(el * em)

    def put(look, lag, value):
        out[look, lag] = value * mask[look, lag].astype(F32)

    own0, own1, opp = sum_energy(mine[64:], 3)
    _, _, _, next0, next1 = sum_energy(mine2[64:], 5)
    put(0, 0, mine[:32] * factor(own0, own1))
    put(0, 1, mine2[:32] * factor(own0, next0))
    put(0, 2, mine2[32:64] * factor(own0, next1))
    b0, b1, bq, bn0, _ = sum_energy(back[96:], 5)
    put(1, 0, back[:32] * factor(bq, b0))
    put(1, 1, back[32:64] * factor(bq, b1))
    put(1, 2, back[64:96] * factor(bq, bn0))
    o0, o1, oo = sum_energy(other[32:], 3)
    own_opp = mine[32:64] * factor(jnp.where(lo, own1, own0), opp)
    other_opp = other[:32] * factor(jnp.where(lo, o0, o1), oo)
    put(0, 3, jnp.where(lo, other_opp, own_opp))
    put(1, 3, jnp.where(lo, own_opp, other_opp))


def after(array, *others):
    return lax.optimization_barrier((array,) + others)[0]


def per_device(images, patch_weight, pair_mask):
    nlook = lax.axis_size("look")
    nswath = lax.axis_size("swath")
    ring = nlook // 2
    edge = lax.axis_index("look") % ring == 0
    tables, inverse_tables = make_tables()

    def over_look(array, to):
        return lax.ppermute(array, "look", [(i, to(i)) for i in range(nlook)])

    def over_x(parts):
        moved = [parts[0]]
        for by in range(1, 4):
            perm = [(i, i // 4 * 4 + (i + by) % 4) for i in range(nswath)]
            moved.append(lax.ppermute(parts[by], "swath", perm))
        return moved

    def over_both(array, to_look, flip):
        perm = [
            (i * nswath + s, to_look(i) * nswath + ((s + nswath // 2) % nswath if flip else s))
            for i in range(nlook)
            for s in range(nswath)
        ]
        return lax.ppermute(array, ("look", "swath"), perm)

    stay = lambda i: i
    ahead = lambda i: (i + 1) % nlook
    behind = lambda i: (i - 1) % nlook
    across = lambda i: (i + ring) % nlook
    turn = lambda i: i // ring * ring + (i - 1) % ring

    sent_a = forward_send((0, 1), images, tables)
    op_a = over_look(sent_a, across)
    sent_b, e0_a, e0_b, e1_a, e1_b, wrapped_a, wrapped_b = forward_rest(images, tables, sent_a)
    op_b = over_look(sent_b, across)
    pl1_a = over_look(wrapped_a, behind)
    q1_a = over_look(e1_a, ahead)
    pl0_a = over_look(jnp.where(edge, op_a, e0_a), turn)
    op_b = after(op_b, pl0_a)
    turn_b = jnp.where(edge, op_b, e0_b)
    pl0_b = over_look(turn_b, turn)
    pl1_b = over_look(after(wrapped_b, turn_b), behind)
    q1_b = over_look(after(e1_b, turn_b), ahead)

    vm = lambda *arrays: [("v", a) for a in arrays]
    common = [("s", patch_weight), ("v", inverse_tables)]
    *early, energy = surfaces(
        early_kernel,
        3,
        common + vm(e0_a, e0_b, e1_a, e1_b, op_a, after(op_b, turn_b, pl1_a, q1_a)),
        [((3, 8, 128), F32)],
        [],
        "surfaces_early",
    )
    early = over_x(early)
    energy = after(energy, *early[1:])
    late = surfaces(
        late_kernel,
        5,
        common + vm(energy, e0_a, e0_b, e1_a, e1_b, q1_a, q1_b, pl0_a, pl0_b, pl1_a, pl1_b),
        [],
        [pltpu.VMEM((5, 8, 128), F32)],
        "surfaces_late",
    )
    late = over_x(late)
    rows = lambda n, t: ((n + EROWS, WIN), t)
    keep, near, opp_same, opp_other = call(
        gather_early_kernel,
        [rows(64, F32), rows(64, BF), rows(32, BF), rows(32, BF)],
        vm(*early),
        [],
        16,
        10,
        "gather_early",
    )
    got = [
        keep,
        over_both(near, stay, True),
        over_both(opp_same, across, False),
        over_both(opp_other, across, True),
    ]
    late[0] = after(late[0], *got)
    keep, near, back_same, back_other = call(
        gather_late_kernel,
        [rows(64, F32), rows(64, BF), rows(96, BF), rows(96, BF)],
        vm(*late),
        [],
        16,
        10,
        "gather_late",
    )
    got += [
        keep,
        over_both(near, stay, True),
        over_both(back_same, behind, False),
        over_both(back_other, behind, True),
    ]
    scale = BAND * math.sqrt(patch_weight.shape[0] * nswath)
    return call(
        functools.partial(final_kernel, scale),
        [((2, 4, 32, WIN), F32)],
        [("s", pair_mask)] + vm(*got),
        [],
        16,
        10,
        "final",
    )[0]


def solution(mesh):
    return jax.shard_map(
        per_device,
        mesh=mesh,
        in_specs=(P("look", "swath", None, None, None), P("swath"), P("look", None)),
        out_specs=P("look", None, "swath", None),
        check_vma=False,
    )
```

```python
import functools
import math

import jax
import jax.numpy as jnp
import numpy as np
from jax import lax
from jax.experimental import pallas as pl
from jax.experimental.pallas import tpu as pltpu
from jax.sharding import PartitionSpec as P

PIX = 512
BAND = 256
WIN = 256
HALF = 256
CHUNK = 2
EROWS = 16
TABLES = 32
REST_LIMIT = 52
BF = jnp.bfloat16
F32 = jnp.float32


def phases(rows, cols):
    phase = (rows[:, None] * cols[None, :]) % PIX
    angle = (2.0 * math.pi / PIX * phase.astype(np.float32)).astype(np.float32)
    return np.cos(angle), np.sin(angle)


def make_tables():
    order = np.concatenate([np.arange(0, BAND, 2), np.arange(1, BAND, 2)])
    n0 = np.arange(HALF)
    left = []
    for parity in range(2):
        ks = np.arange(parity, BAND, 2) - BAND // 2
        re, im = phases(ks, n0)
        im = -im
        left.append(np.block([[re, -im], [im, re]]))
    ts = np.arange(WIN) - WIN // 2
    gre, gim = phases(ts, order - BAND // 2)
    first = np.block([[gre, -gim], [gim, gre]])
    second = np.concatenate([gre, -gim], axis=1)
    cast = lambda a: jnp.asarray(np.asarray(a, np.float32).astype(jnp.bfloat16))
    room = np.zeros((TABLES - 2, 256, 512))
    return cast(np.concatenate([np.stack(left), room])), cast(np.stack([first[:256], first[256:], second]))


def place():
    look = lax.axis_index("look")
    swath = lax.axis_index("swath")
    nlook = lax.axis_size("look")
    return dict(
        lo=(look >= nlook // 2).astype(jnp.int32),
        zero=look == 0,
        last=look == nlook - 1,
        end=lax.rem(look, nlook // 2) == nlook // 2 - 1,
        x=lax.rem(swath, 4),
        yh=swath // 4,
    )


def dot(a, b):
    return jnp.dot(a, b, preferred_element_type=F32)


def dot_nt(a, b):
    return lax.dot_general(a, b, (((1,), (1,)), ((), ())), preferred_element_type=F32)


def butterflies(x):
    x00 = x[:HALF, :HALF].astype(F32)
    x01 = x[:HALF, HALF:].astype(F32)
    x10 = x[HALF:, :HALF].astype(F32)
    x11 = x[HALF:, HALF:].astype(F32)
    a, b = x00 + x10, x01 + x11
    c, d = x00 - x10, x01 - x11
    return [v.astype(BF) for v in (a + b, a - b, c + d, c - d)]


def image_pair(xbuf, at, tab, hbuf, ybuf, store):
    for k in range(2):
        for part in range(2):
            for q, h in enumerate(butterflies(xbuf.at[at + k, part])):
                kp, lp = q // 2, q % 2
                row = 512 * k + 256 * kp
                hbuf[lp, row : row + 256, 256 * part : 256 * part + 256] = h
    for lp in range(2):
        y = dot_nt(hbuf[lp], tab[lp]).astype(BF)
        for k in range(2):
            for kp in range(2):
                block = y[512 * k + 256 * kp : 512 * k + 256 * kp + 256]
                lane = 256 * k + 128 * lp
                ybuf[kp, :256, lane : lane + 128] = block[:, :128]
                ybuf[kp, 256:, lane : lane + 128] = block[:, 128:]
    for kp in range(2):
        spec = dot(tab[kp], ybuf[kp]).astype(BF)
        for k in range(2):
            for part in range(2):
                store(k, part, kp, spec[128 * part : 128 * part + 128, 256 * k : 256 * k + 256])


def image_copies(img, look, patches, xbuf, sems):
    return [
        pltpu.make_async_copy(img.at[look, p], xbuf.at[i], sems.at[i]) for i, p in enumerate(patches)
    ]


def send_kernel(patches, img, tables, out, xbuf, tab, hbuf, ybuf, sems):
    copies = image_copies(img, 1 - place()["lo"], patches, xbuf, sems)
    load = pltpu.make_async_copy(tables.at[pl.ds(0, 2)], tab, sems.at[len(patches)])
    for c in copies[:1] + [load] + copies[1:]:
        c.start()
    for c in copies + [load]:
        c.wait()

    def store(k, part, kp, value):
        out[k, part, 128 * kp : 128 * kp + 128, :] = value

    image_pair(xbuf, 0, tab, hbuf, ybuf, store)


def rest_kernel(
    img, tables, sent_a, e0, e1, wrapped, sent_b, xbuf, tab, hbuf, ybuf, sems
):
    at = place()
    copies = image_copies(img, 1 - at["lo"], (2, 3), xbuf, sems)
    copies += image_copies(img, at["lo"], range(4), xbuf.at[pl.ds(2, 4)], sems.at[pl.ds(2, 4)])
    load = pltpu.make_async_copy(tables.at[pl.ds(0, 2)], tab, sems.at[6])
    for c in copies[:1] + [load] + copies[1:]:
        c.start()
    lo = at["lo"] > 0
    zero = at["zero"]
    load.wait()

    def keep(k, part, kp, value):
        sent_b[k, part, 128 * kp : 128 * kp + 128, :] = value

    for pair in range(3):
        for c in copies[2 * pair : 2 * pair + 2]:
            c.wait()

        def store(k, part, kp, value):
            rows = slice(128 * kp, 128 * kp + 128)
            sent = (sent_a, sent_b)[pair - 1]
            other = sent[k, part, rows, :]
            v0 = jnp.where(lo, other, value)
            v1 = jnp.where(lo, value, other)
            p = 2 * (pair - 1) + k
            e0[p, part, rows, :] = v0
            e1[p, part, rows, :] = v1
            wrapped[p, part, rows, :] = jnp.where(zero, v0, v1)

        image_pair(xbuf, 2 * pair, tab, hbuf.at[pair], ybuf.at[pair], store if pair else keep)


VM = pl.BlockSpec(memory_space=pltpu.VMEM)
SM = pl.BlockSpec(memory_space=pltpu.SMEM)
ANY = pl.BlockSpec(memory_space=pl.ANY)


def call(kernel, outs, ins, scratch, limit, flops, name):
    specs = []
    for kind, _ in ins:
        specs.append({"s": SM, "v": VM, "a": ANY}[kind])
    return pl.pallas_call(
        kernel,
        out_shape=[jax.ShapeDtypeStruct(s, t) for s, t in outs],
        in_specs=specs,
        out_specs=[VM] * len(outs),
        scratch_shapes=scratch,
        compiler_params=pltpu.CompilerParams(vmem_limit_bytes=limit * 2**20),
        cost_estimate=pl.CostEstimate(flops=flops * 10**6, bytes_accessed=2**20, transcendentals=0),
        name=name,
    )(*[a for _, a in ins])


def forward_send(patches, images, tables):
    return call(
        functools.partial(send_kernel, patches),
        [((2, 2, BAND, BAND), BF)],
        [("a", images), ("a", tables)],
        [
            pltpu.VMEM((2, 2, PIX, PIX), BF),
            pltpu.VMEM((2, 256, 512), BF),
            pltpu.VMEM((2, 1024, 512), BF),
            pltpu.VMEM((2, 512, 512), BF),
            pltpu.SemaphoreType.DMA((3,)),
        ],
        57,
        1200,
        "forward_send",
    )[0]


def forward_rest(images, tables, sent_a):
    return call(
        rest_kernel,
        [((4, 2, BAND, BAND), BF)] * 3 + [((2, 2, BAND, BAND), BF)],
        [("a", images), ("a", tables), ("v", sent_a)],
        [
            pltpu.VMEM((6, 2, PIX, PIX), BF),
            pltpu.VMEM((2, 256, 512), BF),
            pltpu.VMEM((3, 2, 1024, 512), BF),
            pltpu.VMEM((3, 2, 512, 512), BF),
            pltpu.SemaphoreType.DMA((7,)),
        ],
        REST_LIMIT,
        3600,
        "forward_rest",
    )


def load_block(ref, p, row, lane):
    return [ref[p, part, pl.ds(row, 16), lane].astype(F32) for part in range(2)]


def accumulate(acc, i, l, m):
    acc[2 * i] = acc[2 * i] + (l[0] * m[0] + l[1] * m[1])
    acc[2 * i + 1] = acc[2 * i + 1] + (l[1] * m[0] - l[0] * m[1])


def add_energy(energy, i, w, s):
    energy[i] = energy[i] + w * (s[0] * s[0] + s[1] * s[1])


def pick(cond, a, b):
    return [jnp.where(cond, u, v) for u, v in zip(a, b)]


def inverse(tab, cross, surf, pairs, at):
    for i in range(pairs):
        shifted = dot(tab[0], cross[i]).astype(BF)
        low = dot(tab[1], cross[i]).astype(BF)
        surf[at + i] = (dot_nt(shifted, tab[2, :, :BAND]) + dot_nt(low, tab[2, :, BAND:])).astype(BF)


def emit(surf, pairs, outs, erows):
    x = place()["x"]
    for slot, out in enumerate(outs):
        dest = lax.rem(x + slot, 4)
        for yh in range(2):
            start = pl.multiple_of((4 * yh + dest) * 32, 32)
            for i in range(pairs):
                out[yh, 32 * i : 32 * i + 32, :] = surf[i, pl.ds(start, 32), :]
            out[yh, 32 * pairs :, :] = erows


def split(value):
    hi = value.astype(BF).astype(F32)
    return hi, (value - hi).astype(BF).astype(F32)


def energy_rows(values):
    his, los = zip(*[split(v) for v in values])
    pad = [jnp.zeros_like(values[0])] * (EROWS - 2 * len(values))
    return jnp.concatenate(list(his) + list(los) + pad, axis=0).astype(BF)


def total_rows(energy_sum, count):
    totals = []
    for i in range(count):
        total = jnp.sum(jnp.sum(energy_sum[i], axis=1, keepdims=True), axis=0, keepdims=True)
        totals.append(jnp.broadcast_to(total, (1, WIN)))
    return energy_rows(totals)


def blocks(body):
    @pl.loop(0, BAND // 16)
    def _(block):
        row = pl.multiple_of(block * 16, 16)
        rowi = pl.multiple_of(block * 16 + BAND, 16)
        for half in range(2):
            body(row, rowi, slice(128 * half, 128 * half + 128))


def zeros(count):
    return [jnp.zeros((16, 128), F32)] * count


def early_kernel(weight, tab, e0, e1, op_a, op_b, surf, energy_out, cross):
    lo = place()["lo"] > 0
    energy_out[...] = jnp.zeros_like(energy_out)

    def body(row, rowi, lane):
        acc, energy = zeros(4), zeros(3)
        for p in range(4):
            w = weight[p]
            own0, own1 = load_block(e0, p, row, lane), load_block(e1, p, row, lane)
            opp = load_block((op_a, op_b)[p // 2], p % 2, row, lane)
            for i, v in enumerate((own0, own1, opp)):
                add_energy(energy, i, w, v)
            accumulate(acc, 0, [w * v for v in own0], own1)
            accumulate(acc, 1, [w * v for v in pick(lo, own1, own0)], opp)
        for i in range(2):
            cross[i, pl.ds(row, 16), lane] = acc[2 * i].astype(BF)
            cross[i, pl.ds(rowi, 16), lane] = acc[2 * i + 1].astype(BF)
        cross[2, pl.ds(row, 16), lane] = acc[2].astype(BF)
        cross[2, pl.ds(rowi, 16), lane] = (-acc[3]).astype(BF)
        for i in range(3):
            energy_out[i] += energy[i][:8] + energy[i][8:]

    blocks(body)
    inverse(tab, cross, surf, 3, 0)


def late_kernel(
    weight, tab, early, energy_in, e0, e1, q1, pl0, pl1, turn_a, turn_b, s0, s1, s2, s3, cross, surf, energy_sum
):
    at = place()
    swapped, end = at["last"], at["end"]
    energy_sum[0:3] = energy_in[...]
    energy_sum[3:6] = jnp.zeros((3, 8, 128), F32)

    def body(row, rowi, lane):
        acc, energy = zeros(10), zeros(3)
        for p in range(4):
            w = weight[p]
            own0, own1 = load_block(e0, p, row, lane), load_block(e1, p, row, lane)
            prev = load_block(q1, p, row, lane)
            turned = (turn_a, turn_b)[p // 2]
            a = [
                jnp.where(end, turned[p % 2, part, pl.ds(row, 16), lane], pl0[p, part, pl.ds(row, 16), lane]).astype(F32)
                for part in range(2)
            ]
            b = load_block(pl1, p, row, lane)
            next0, next1 = pick(swapped, b, a), pick(swapped, a, b)
            for i, v in enumerate((prev, next0, next1)):
                add_energy(energy, i, w, v)
            w0 = [w * v for v in own0]
            wq = [w * v for v in prev]
            for i, (l, m) in enumerate(
                ((w0, next0), (w0, next1), (wq, own0), (wq, own1), (wq, next0))
            ):
                accumulate(acc, i, l, m)
        for i in range(5):
            cross[i, pl.ds(row, 16), lane] = acc[2 * i].astype(BF)
            cross[i, pl.ds(rowi, 16), lane] = acc[2 * i + 1].astype(BF)
        for i in range(3):
            energy_sum[3 + i] += energy[i][:8] + energy[i][8:]

    blocks(body)
    surf[0:3] = early[...]
    inverse(tab, cross, surf, 5, 3)
    emit(surf, 8, (s0, s1, s2, s3), total_rows(energy_sum, 6))


def surfaces(kernel, pairs, outs, ins, scratch, name):
    return call(
        kernel,
        outs,
        ins,
        [pltpu.VMEM((pairs, 2 * BAND, BAND), BF)] + scratch,
        28,
        250 * pairs,
        name,
    )


def sum_energy(block, count):
    return [block[i : i + 1] + block[count + i : count + i + 1] for i in range(count)]


def add_parts(parts, h):
    a, b, c, d = [r[h].astype(F32) for r in parts]
    return (a + b) + (c + d)


def gather_kernel(a, b, c, d, keep, near, back_same, back_other, opp_same, opp_other):
    yh = place()["yh"]
    for h, (near_out, back_out, opp_out) in (
        (yh, (keep, back_same, opp_same)),
        (1 - yh, (near, back_other, opp_other)),
    ):
        total = add_parts((a, b, c, d), h)
        erows = energy_rows(sum_energy(total[256:], 6))
        near_out[0:64] = total[0:64].astype(near_out.dtype)
        near_out[64:128] = total[96:160].astype(near_out.dtype)
        near_out[128:] = erows.astype(near_out.dtype)
        back_out[0:96] = total[160:256].astype(BF)
        back_out[96:] = erows
        opp_out[0:32] = total[64:96].astype(BF)
        opp_out[32:] = erows


def final_kernel(scale, mask, keep, near, back_a, back_b, opp_a, opp_b, out):
    lo = place()["lo"] > 0
    mine = keep[...] + near[...].astype(F32)
    back = back_a[...].astype(F32) + back_b[...].astype(F32)
    other = opp_a[...].astype(F32) + opp_b[...].astype(F32)

    def factor(el, em):
        return scale / jnp.sqrt(el * em)

    def put(look, lag, value):
        out[look, lag] = value * mask[look, lag].astype(F32)

    own0, own1, opp, _, next0, next1 = sum_energy(mine[128:], 6)
    put(0, 0, mine[:32] * factor(own0, own1))
    put(0, 1, mine[64:96] * factor(own0, next0))
    put(0, 2, mine[96:128] * factor(own0, next1))
    b0, b1, _, bq, bn0, _ = sum_energy(back[96:], 6)
    put(1, 0, back[:32] * factor(bq, b0))
    put(1, 1, back[32:64] * factor(bq, b1))
    put(1, 2, back[64:96] * factor(bq, bn0))
    o0, o1, oo, _, _, _ = sum_energy(other[32:], 6)
    own_opp = mine[32:64] * factor(jnp.where(lo, own1, own0), opp)
    other_opp = other[:32] * factor(jnp.where(lo, o0, o1), oo)
    put(0, 3, jnp.where(lo, other_opp, own_opp))
    put(1, 3, jnp.where(lo, own_opp, other_opp))


def after(array, *others):
    return lax.optimization_barrier((array,) + others)[0]


def per_device(images, patch_weight, pair_mask):
    nlook = lax.axis_size("look")
    nswath = lax.axis_size("swath")
    ring = nlook // 2
    tables, inverse_tables = make_tables()

    def over_look(array, to):
        return lax.ppermute(array, "look", [(i, to(i)) for i in range(nlook)])

    def over_x(parts):
        moved = [parts[0]]
        for by in range(1, 4):
            perm = [(i, i // 4 * 4 + (i + by) % 4) for i in range(nswath)]
            moved.append(lax.ppermute(parts[by], "swath", perm))
        return moved

    def over_both(array, to_look, flip):
        perm = [
            (i * nswath + s, to_look(i) * nswath + ((s + nswath // 2) % nswath if flip else s))
            for i in range(nlook)
            for s in range(nswath)
        ]
        return lax.ppermute(array, ("look", "swath"), perm)

    stay = lambda i: i
    ahead = lambda i: (i + 1) % nlook
    behind = lambda i: (i - 1) % nlook
    across = lambda i: (i + ring) % nlook
    turn = lambda i: i // ring * ring + (i - 1) % ring

    sent_a = forward_send((0, 1), images, tables)
    op_a = over_look(sent_a, across)
    e0, e1, wrapped, sent_b = forward_rest(images, tables, sent_a)
    op_b = over_look(sent_b, across)
    pl0 = lax.ppermute(e0, "look", [(i, turn(i)) for i in range(nlook) if i % ring])
    edges = [(i, turn(i)) for i in range(nlook) if i % ring == 0]
    turn_a = lax.ppermute(op_a, "look", edges)
    op_b = after(op_b, pl0, turn_a)
    turn_b = lax.ppermute(op_b, "look", edges)
    pl1 = over_look(after(wrapped, op_b), behind)
    q1 = over_look(after(e1, op_b), ahead)

    vm = lambda *arrays: [("v", a) for a in arrays]
    common = [("s", patch_weight), ("v", inverse_tables)]
    surf, energy = surfaces(
        early_kernel,
        3,
        [((3, WIN, WIN), BF), ((3, 8, 128), F32)],
        common + vm(e0, e1, op_a, op_b),
        [],
        "surfaces_early",
    )
    parts = surfaces(
        late_kernel,
        5,
        [((2, 8 * 32 + EROWS, WIN), BF)] * 4,
        common + vm(surf, energy, e0, e1, q1, pl0, pl1, turn_a, turn_b),
        [pltpu.VMEM((8, WIN, WIN), BF), pltpu.VMEM((6, 8, 128), F32)],
        "surfaces_late",
    )
    rows = lambda n, t: ((n + EROWS, WIN), t)
    keep, near, back_same, back_other, opp_same, opp_other = call(
        gather_kernel,
        [rows(128, F32), rows(128, BF), rows(96, BF), rows(96, BF), rows(32, BF), rows(32, BF)],
        vm(*over_x(parts)),
        [],
        16,
        10,
        "gather",
    )
    got = (
        keep,
        over_both(near, stay, True),
        over_both(back_same, behind, False),
        over_both(back_other, behind, True),
        over_both(opp_same, across, False),
        over_both(opp_other, across, True),
    )
    scale = BAND * math.sqrt(patch_weight.shape[0] * nswath)
    return call(
        functools.partial(final_kernel, scale),
        [((2, 4, 32, WIN), F32)],
        [("s", pair_mask)] + vm(*got),
        [],
        16,
        10,
        "final",
    )[0]


def solution(mesh):
    return jax.shard_map(
        per_device,
        mesh=mesh,
        in_specs=(P("look", "swath", None, None, None), P("swath"), P("look", None)),
        out_specs=P("look", None, "swath", None),
        check_vma=False,
    )
```

```python
import functools
import math

import jax
import jax.numpy as jnp
import numpy as np
from jax import lax
from jax.experimental import pallas as pl
from jax.experimental.pallas import tpu as pltpu
from jax.sharding import PartitionSpec as P

PIX = 512
BAND = 256
WIN = 256
HALF = 256
CHUNK = 2
EROWS = 16
TABLES = 32
REST_LIMIT = 52
BF = jnp.bfloat16
F32 = jnp.float32


def phases(rows, cols):
    phase = (rows[:, None] * cols[None, :]) % PIX
    angle = (2.0 * math.pi / PIX * phase.astype(np.float32)).astype(np.float32)
    return np.cos(angle), np.sin(angle)


def make_tables():
    order = np.concatenate([np.arange(0, BAND, 2), np.arange(1, BAND, 2)])
    n0 = np.arange(HALF)
    left = []
    for parity in range(2):
        ks = np.arange(parity, BAND, 2) - BAND // 2
        re, im = phases(ks, n0)
        im = -im
        left.append(np.block([[re, -im], [im, re]]))
    ts = np.arange(WIN) - WIN // 2
    gre, gim = phases(ts, order - BAND // 2)
    first = np.block([[gre, -gim], [gim, gre]])
    second = np.concatenate([gre, -gim], axis=1)
    cast = lambda a: jnp.asarray(np.asarray(a, np.float32).astype(jnp.bfloat16))
    room = np.zeros((TABLES - 2, 256, 512))
    return cast(np.concatenate([np.stack(left), room])), cast(np.stack([first[:256], first[256:], second]))


def place():
    look = lax.axis_index("look")
    swath = lax.axis_index("swath")
    nlook = lax.axis_size("look")
    return dict(
        lo=(look >= nlook // 2).astype(jnp.int32),
        zero=look == 0,
        last=look == nlook - 1,
        end=lax.rem(look, nlook // 2) == nlook // 2 - 1,
        x=lax.rem(swath, 4),
        yh=swath // 4,
    )


def dot(a, b):
    return jnp.dot(a, b, preferred_element_type=F32)


def dot_nt(a, b):
    return lax.dot_general(a, b, (((1,), (1,)), ((), ())), preferred_element_type=F32)


def butterflies(x):
    x00 = x[:HALF, :HALF].astype(F32)
    x01 = x[:HALF, HALF:].astype(F32)
    x10 = x[HALF:, :HALF].astype(F32)
    x11 = x[HALF:, HALF:].astype(F32)
    a, b = x00 + x10, x01 + x11
    c, d = x00 - x10, x01 - x11
    return [v.astype(BF) for v in (a + b, a - b, c + d, c - d)]


def image_pair(xbuf, at, tab, hbuf, ybuf, store):
    for k in range(2):
        for part in range(2):
            for q, h in enumerate(butterflies(xbuf.at[at + k, part])):
                kp, lp = q // 2, q % 2
                row = 512 * k + 256 * kp
                hbuf[lp, row : row + 256, 256 * part : 256 * part + 256] = h
    for lp in range(2):
        y = dot_nt(hbuf[lp], tab[lp]).astype(BF)
        for k in range(2):
            for kp in range(2):
                block = y[512 * k + 256 * kp : 512 * k + 256 * kp + 256]
                lane = 256 * k + 128 * lp
                ybuf[kp, :256, lane : lane + 128] = block[:, :128]
                ybuf[kp, 256:, lane : lane + 128] = block[:, 128:]
    for kp in range(2):
        spec = dot(tab[kp], ybuf[kp]).astype(BF)
        for k in range(2):
            for part in range(2):
                store(k, part, kp, spec[128 * part : 128 * part + 128, 256 * k : 256 * k + 256])


def image_copies(img, look, patches, xbuf, sems):
    return [
        pltpu.make_async_copy(img.at[look, p], xbuf.at[i], sems.at[i]) for i, p in enumerate(patches)
    ]


def send_kernel(patches, img, tables, out, xbuf, tab, hbuf, ybuf, sems):
    copies = image_copies(img, 1 - place()["lo"], patches, xbuf, sems)
    load = pltpu.make_async_copy(tables.at[pl.ds(0, 2)], tab, sems.at[len(patches)])
    for c in copies[:1] + [load] + copies[1:]:
        c.start()
    for c in copies + [load]:
        c.wait()

    def store(k, part, kp, value):
        out[k, part, 128 * kp : 128 * kp + 128, :] = value

    image_pair(xbuf, 0, tab, hbuf, ybuf, store)


def rest_kernel(
    img, tables, sent_a, e0, e1, wrapped, sent_b, xbuf, tab, hbuf, ybuf, sems
):
    at = place()
    copies = image_copies(img, 1 - at["lo"], (2, 3), xbuf, sems)
    copies += image_copies(img, at["lo"], range(4), xbuf.at[pl.ds(2, 4)], sems.at[pl.ds(2, 4)])
    load = pltpu.make_async_copy(tables.at[pl.ds(0, 2)], tab, sems.at[6])
    for c in copies[:1] + [load] + copies[1:]:
        c.start()
    lo = at["lo"] > 0
    zero = at["zero"]
    load.wait()

    def keep(k, part, kp, value):
        sent_b[k, part, 128 * kp : 128 * kp + 128, :] = value

    for pair in range(3):
        for c in copies[2 * pair : 2 * pair + 2]:
            c.wait()

        def store(k, part, kp, value):
            rows = slice(128 * kp, 128 * kp + 128)
            sent = (sent_a, sent_b)[pair - 1]
            other = sent[k, part, rows, :]
            v0 = jnp.where(lo, other, value)
            v1 = jnp.where(lo, value, other)
            p = 2 * (pair - 1) + k
            e0[p, part, rows, :] = v0
            e1[p, part, rows, :] = v1
            wrapped[p, part, rows, :] = jnp.where(zero, v0, v1)

        image_pair(xbuf, 2 * pair, tab, hbuf.at[pair], ybuf.at[pair], store if pair else keep)


VM = pl.BlockSpec(memory_space=pltpu.VMEM)
SM = pl.BlockSpec(memory_space=pltpu.SMEM)
ANY = pl.BlockSpec(memory_space=pl.ANY)


def call(kernel, outs, ins, scratch, limit, flops, name):
    specs = []
    for kind, _ in ins:
        specs.append({"s": SM, "v": VM, "a": ANY}[kind])
    return pl.pallas_call(
        kernel,
        out_shape=[jax.ShapeDtypeStruct(s, t) for s, t in outs],
        in_specs=specs,
        out_specs=[VM] * len(outs),
        scratch_shapes=scratch,
        compiler_params=pltpu.CompilerParams(vmem_limit_bytes=limit * 2**20),
        cost_estimate=pl.CostEstimate(flops=flops * 10**6, bytes_accessed=2**20, transcendentals=0),
        name=name,
    )(*[a for _, a in ins])


def forward_send(patches, images, tables):
    return call(
        functools.partial(send_kernel, patches),
        [((2, 2, BAND, BAND), BF)],
        [("a", images), ("a", tables)],
        [
            pltpu.VMEM((2, 2, PIX, PIX), BF),
            pltpu.VMEM((2, 256, 512), BF),
            pltpu.VMEM((2, 1024, 512), BF),
            pltpu.VMEM((2, 512, 512), BF),
            pltpu.SemaphoreType.DMA((3,)),
        ],
        57,
        1200,
        "forward_send",
    )[0]


def forward_rest(images, tables, sent_a):
    return call(
        rest_kernel,
        [((4, 2, BAND, BAND), BF)] * 3 + [((2, 2, BAND, BAND), BF)],
        [("a", images), ("a", tables), ("v", sent_a)],
        [
            pltpu.VMEM((6, 2, PIX, PIX), BF),
            pltpu.VMEM((2, 256, 512), BF),
            pltpu.VMEM((3, 2, 1024, 512), BF),
            pltpu.VMEM((3, 2, 512, 512), BF),
            pltpu.SemaphoreType.DMA((7,)),
        ],
        REST_LIMIT,
        3600,
        "forward_rest",
    )


def load_block(ref, p, row, lane):
    return [ref[p, part, pl.ds(row, 16), lane].astype(F32) for part in range(2)]


def accumulate(acc, i, l, m):
    acc[2 * i] = acc[2 * i] + (l[0] * m[0] + l[1] * m[1])
    acc[2 * i + 1] = acc[2 * i + 1] + (l[1] * m[0] - l[0] * m[1])


def add_energy(energy, i, w, s):
    energy[i] = energy[i] + w * (s[0] * s[0] + s[1] * s[1])


def pick(cond, a, b):
    return [jnp.where(cond, u, v) for u, v in zip(a, b)]


def inverse(tab, cross, surf, pairs, at):
    for i in range(pairs):
        shifted = dot(tab[0], cross[i]).astype(BF)
        low = dot(tab[1], cross[i]).astype(BF)
        surf[at + i] = (dot_nt(shifted, tab[2, :, :BAND]) + dot_nt(low, tab[2, :, BAND:])).astype(BF)


def emit(surf, pairs, outs, erows):
    x = place()["x"]
    for slot, out in enumerate(outs):
        dest = lax.rem(x + slot, 4)
        for yh in range(2):
            start = pl.multiple_of((4 * yh + dest) * 32, 32)
            for i in range(pairs):
                out[yh, 32 * i : 32 * i + 32, :] = surf[i, pl.ds(start, 32), :]
            out[yh, 32 * pairs :, :] = erows


def split(value):
    hi = value.astype(BF).astype(F32)
    return hi, (value - hi).astype(BF).astype(F32)


def energy_rows(values):
    his, los = zip(*[split(v) for v in values])
    pad = [jnp.zeros_like(values[0])] * (EROWS - 2 * len(values))
    return jnp.concatenate(list(his) + list(los) + pad, axis=0).astype(BF)


def total_rows(energy_sum, count):
    totals = []
    for i in range(count):
        total = jnp.sum(jnp.sum(energy_sum[i], axis=1, keepdims=True), axis=0, keepdims=True)
        totals.append(jnp.broadcast_to(total, (1, WIN)))
    return energy_rows(totals)


def blocks(body):
    @pl.loop(0, BAND // 16)
    def _(block):
        row = pl.multiple_of(block * 16, 16)
        rowi = pl.multiple_of(block * 16 + BAND, 16)
        for half in range(2):
            body(row, rowi, slice(128 * half, 128 * half + 128))


def zeros(count):
    return [jnp.zeros((16, 128), F32)] * count


def early_kernel(weight, tab, e0, e1, op_a, op_b, surf, energy_out, cross):
    lo = place()["lo"] > 0
    energy_out[...] = jnp.zeros_like(energy_out)

    def body(row, rowi, lane):
        acc, energy = zeros(4), zeros(3)
        for p in range(4):
            w = weight[p]
            own0, own1 = load_block(e0, p, row, lane), load_block(e1, p, row, lane)
            opp = load_block((op_a, op_b)[p // 2], p % 2, row, lane)
            for i, v in enumerate((own0, own1, opp)):
                add_energy(energy, i, w, v)
            accumulate(acc, 0, [w * v for v in own0], own1)
            accumulate(acc, 1, [w * v for v in pick(lo, own1, own0)], opp)
        for i in range(2):
            cross[i, pl.ds(row, 16), lane] = acc[2 * i].astype(BF)
            cross[i, pl.ds(rowi, 16), lane] = acc[2 * i + 1].astype(BF)
        cross[2, pl.ds(row, 16), lane] = acc[2].astype(BF)
        cross[2, pl.ds(rowi, 16), lane] = (-acc[3]).astype(BF)
        for i in range(3):
            energy_out[i] += energy[i][:8] + energy[i][8:]

    blocks(body)
    inverse(tab, cross, surf, 3, 0)


def late_kernel(
    weight, tab, early, energy_in, e0, e1, q1, pl0, pl1, turn_a, turn_b, s0, s1, s2, s3, cross, surf, energy_sum
):
    at = place()
    swapped, end = at["last"], at["end"]
    energy_sum[0:3] = energy_in[...]
    energy_sum[3:6] = jnp.zeros((3, 8, 128), F32)

    def body(row, rowi, lane):
        acc, energy = zeros(10), zeros(3)
        for p in range(4):
            w = weight[p]
            own0, own1 = load_block(e0, p, row, lane), load_block(e1, p, row, lane)
            prev = load_block(q1, p, row, lane)
            turned = (turn_a, turn_b)[p // 2]
            a = [
                jnp.where(end, turned[p % 2, part, pl.ds(row, 16), lane], pl0[p, part, pl.ds(row, 16), lane]).astype(F32)
                for part in range(2)
            ]
            b = load_block(pl1, p, row, lane)
            next0, next1 = pick(swapped, b, a), pick(swapped, a, b)
            for i, v in enumerate((prev, next0, next1)):
                add_energy(energy, i, w, v)
            w0 = [w * v for v in own0]
            wq = [w * v for v in prev]
            for i, (l, m) in enumerate(
                ((w0, next0), (w0, next1), (wq, own0), (wq, own1), (wq, next0))
            ):
                accumulate(acc, i, l, m)
        for i in range(5):
            cross[i, pl.ds(row, 16), lane] = acc[2 * i].astype(BF)
            cross[i, pl.ds(rowi, 16), lane] = acc[2 * i + 1].astype(BF)
        for i in range(3):
            energy_sum[3 + i] += energy[i][:8] + energy[i][8:]

    blocks(body)
    surf[0:3] = early[...]
    inverse(tab, cross, surf, 5, 3)
    emit(surf, 8, (s0, s1, s2, s3), total_rows(energy_sum, 6))


def surfaces(kernel, pairs, outs, ins, scratch, name):
    return call(
        kernel,
        outs,
        ins,
        [pltpu.VMEM((pairs, 2 * BAND, BAND), BF)] + scratch,
        28,
        250 * pairs,
        name,
    )


def sum_energy(block, count):
    return [block[i : i + 1] + block[count + i : count + i + 1] for i in range(count)]


def add_parts(parts, h):
    a, b, c, d = [r[h].astype(F32) for r in parts]
    return (a + b) + (c + d)


def gather_kernel(a, b, c, d, keep, near, back_same, back_other, opp_same, opp_other):
    yh = place()["yh"]
    for h, (near_out, back_out, opp_out) in (
        (yh, (keep, back_same, opp_same)),
        (1 - yh, (near, back_other, opp_other)),
    ):
        total = add_parts((a, b, c, d), h)
        erows = energy_rows(sum_energy(total[256:], 6))
        near_out[0:64] = total[0:64].astype(near_out.dtype)
        near_out[64:128] = total[96:160].astype(near_out.dtype)
        near_out[128:] = erows.astype(near_out.dtype)
        back_out[0:96] = total[160:256].astype(BF)
        back_out[96:] = erows
        opp_out[0:32] = total[64:96].astype(BF)
        opp_out[32:] = erows


def final_kernel(scale, mask, keep, near, back_a, back_b, opp_a, opp_b, out):
    lo = place()["lo"] > 0
    mine = keep[...] + near[...].astype(F32)
    back = back_a[...].astype(F32) + back_b[...].astype(F32)
    other = opp_a[...].astype(F32) + opp_b[...].astype(F32)

    def factor(el, em):
        return scale / jnp.sqrt(el * em)

    def put(look, lag, value):
        out[look, lag] = value * mask[look, lag].astype(F32)

    own0, own1, opp, _, next0, next1 = sum_energy(mine[128:], 6)
    put(0, 0, mine[:32] * factor(own0, own1))
    put(0, 1, mine[64:96] * factor(own0, next0))
    put(0, 2, mine[96:128] * factor(own0, next1))
    b0, b1, _, bq, bn0, _ = sum_energy(back[96:], 6)
    put(1, 0, back[:32] * factor(bq, b0))
    put(1, 1, back[32:64] * factor(bq, b1))
    put(1, 2, back[64:96] * factor(bq, bn0))
    o0, o1, oo, _, _, _ = sum_energy(other[32:], 6)
    own_opp = mine[32:64] * factor(jnp.where(lo, own1, own0), opp)
    other_opp = other[:32] * factor(jnp.where(lo, o0, o1), oo)
    put(0, 3, jnp.where(lo, other_opp, own_opp))
    put(1, 3, jnp.where(lo, own_opp, other_opp))


def after(array, *others):
    return lax.optimization_barrier((array,) + others)[0]


def per_device(images, patch_weight, pair_mask):
    nlook = lax.axis_size("look")
    nswath = lax.axis_size("swath")
    ring = nlook // 2
    tables, inverse_tables = make_tables()

    def over_look(array, to):
        return lax.ppermute(array, "look", [(i, to(i)) for i in range(nlook)])

    def over_x(parts):
        moved = [parts[0]]
        for by in range(1, 4):
            perm = [(i, i // 4 * 4 + (i + by) % 4) for i in range(nswath)]
            moved.append(lax.ppermute(parts[by], "swath", perm))
        return moved

    def over_both(array, to_look, flip):
        perm = [
            (i * nswath + s, to_look(i) * nswath + ((s + nswath // 2) % nswath if flip else s))
            for i in range(nlook)
            for s in range(nswath)
        ]
        return lax.ppermute(array, ("look", "swath"), perm)

    stay = lambda i: i
    ahead = lambda i: (i + 1) % nlook
    behind = lambda i: (i - 1) % nlook
    across = lambda i: (i + ring) % nlook
    turn = lambda i: i // ring * ring + (i - 1) % ring

    sent_a = forward_send((0, 1), images, tables)
    op_a = over_look(sent_a, across)
    e0, e1, wrapped, sent_b = forward_rest(images, tables, sent_a)
    op_b = over_look(sent_b, across)
    pl0 = lax.ppermute(e0, "look", [(i, turn(i)) for i in range(nlook) if i % ring])
    edges = [(i, turn(i)) for i in range(nlook) if i % ring == 0]
    turn_a = lax.ppermute(op_a, "look", edges)
    op_b = after(op_b, pl0, turn_a)
    turn_b = lax.ppermute(op_b, "look", edges)
    pl1 = over_look(after(wrapped, op_a), behind)
    q1 = over_look(after(e1, op_a), ahead)

    vm = lambda *arrays: [("v", a) for a in arrays]
    common = [("s", patch_weight), ("v", inverse_tables)]
    surf, energy = surfaces(
        early_kernel,
        3,
        [((3, WIN, WIN), BF), ((3, 8, 128), F32)],
        common + vm(e0, e1, op_a, op_b),
        [],
        "surfaces_early",
    )
    parts = surfaces(
        late_kernel,
        5,
        [((2, 8 * 32 + EROWS, WIN), BF)] * 4,
        common + vm(surf, energy, e0, e1, q1, pl0, pl1, turn_a, turn_b),
        [pltpu.VMEM((8, WIN, WIN), BF), pltpu.VMEM((6, 8, 128), F32)],
        "surfaces_late",
    )
    rows = lambda n, t: ((n + EROWS, WIN), t)
    keep, near, back_same, back_other, opp_same, opp_other = call(
        gather_kernel,
        [rows(128, F32), rows(128, BF), rows(96, BF), rows(96, BF), rows(32, BF), rows(32, BF)],
        vm(*over_x(parts)),
        [],
        16,
        10,
        "gather",
    )
    got = (
        keep,
        over_both(near, stay, True),
        over_both(back_same, behind, False),
        over_both(back_other, behind, True),
        over_both(opp_same, across, False),
        over_both(opp_other, across, True),
    )
    scale = BAND * math.sqrt(patch_weight.shape[0] * nswath)
    return call(
        functools.partial(final_kernel, scale),
        [((2, 4, 32, WIN), F32)],
        [("s", pair_mask)] + vm(*got),
        [],
        16,
        10,
        "final",
    )[0]


def solution(mesh):
    return jax.shard_map(
        per_device,
        mesh=mesh,
        in_specs=(P("look", "swath", None, None, None), P("swath"), P("look", None)),
        out_specs=P("look", None, "swath", None),
        check_vma=False,
    )
```

```python
import functools
import math

import jax
import jax.numpy as jnp
import numpy as np
from jax import lax
from jax.experimental import pallas as pl
from jax.experimental.pallas import tpu as pltpu
from jax.sharding import PartitionSpec as P

PIX = 512
BAND = 256
WIN = 256
HALF = 256
CHUNK = 2
EROWS = 16
TABLES = 32
REST_LIMIT = 52
BF = jnp.bfloat16
F32 = jnp.float32


def phases(rows, cols):
    phase = (rows[:, None] * cols[None, :]) % PIX
    angle = (2.0 * math.pi / PIX * phase.astype(np.float32)).astype(np.float32)
    return np.cos(angle), np.sin(angle)


def make_tables():
    order = np.concatenate([np.arange(0, BAND, 2), np.arange(1, BAND, 2)])
    n0 = np.arange(HALF)
    left = []
    for parity in range(2):
        ks = np.arange(parity, BAND, 2) - BAND // 2
        re, im = phases(ks, n0)
        im = -im
        left.append(np.block([[re, -im], [im, re]]))
    ts = np.arange(WIN) - WIN // 2
    gre, gim = phases(ts, order - BAND // 2)
    first = np.block([[gre, -gim], [gim, gre]])
    second = np.concatenate([gre, -gim], axis=1)
    cast = lambda a: jnp.asarray(np.asarray(a, np.float32).astype(jnp.bfloat16))
    room = np.zeros((TABLES - 2, 256, 512))
    return cast(np.concatenate([np.stack(left), room])), cast(np.stack([first[:256], first[256:], second]))


def place():
    look = lax.axis_index("look")
    swath = lax.axis_index("swath")
    nlook = lax.axis_size("look")
    return dict(
        lo=(look >= nlook // 2).astype(jnp.int32),
        zero=look == 0,
        last=look == nlook - 1,
        end=lax.rem(look, nlook // 2) == nlook // 2 - 1,
        x=lax.rem(swath, 4),
        yh=swath // 4,
    )


def dot(a, b):
    return jnp.dot(a, b, preferred_element_type=F32)


def dot_nt(a, b):
    return lax.dot_general(a, b, (((1,), (1,)), ((), ())), preferred_element_type=F32)


def butterflies(x):
    x00 = x[:HALF, :HALF].astype(F32)
    x01 = x[:HALF, HALF:].astype(F32)
    x10 = x[HALF:, :HALF].astype(F32)
    x11 = x[HALF:, HALF:].astype(F32)
    a, b = x00 + x10, x01 + x11
    c, d = x00 - x10, x01 - x11
    return [v.astype(BF) for v in (a + b, a - b, c + d, c - d)]


def image_pair(xbuf, at, tab, hbuf, ybuf, store):
    for k in range(2):
        for part in range(2):
            for q, h in enumerate(butterflies(xbuf.at[at + k, part])):
                kp, lp = q // 2, q % 2
                row = 512 * k + 256 * kp
                hbuf[lp, row : row + 256, 256 * part : 256 * part + 256] = h
    for lp in range(2):
        y = dot_nt(hbuf[lp], tab[lp]).astype(BF)
        for k in range(2):
            for kp in range(2):
                block = y[512 * k + 256 * kp : 512 * k + 256 * kp + 256]
                lane = 256 * k + 128 * lp
                ybuf[kp, :256, lane : lane + 128] = block[:, :128]
                ybuf[kp, 256:, lane : lane + 128] = block[:, 128:]
    for kp in range(2):
        spec = dot(tab[kp], ybuf[kp]).astype(BF)
        for k in range(2):
            for part in range(2):
                store(k, part, kp, spec[128 * part : 128 * part + 128, 256 * k : 256 * k + 256])


def image_copies(img, look, patches, xbuf, sems):
    return [
        pltpu.make_async_copy(img.at[look, p], xbuf.at[i], sems.at[i]) for i, p in enumerate(patches)
    ]


def send_kernel(patches, img, tables, out, xbuf, tab, hbuf, ybuf, sems):
    copies = image_copies(img, 1 - place()["lo"], patches, xbuf, sems)
    load = pltpu.make_async_copy(tables.at[pl.ds(0, 2)], tab, sems.at[len(patches)])
    for c in copies[:1] + [load] + copies[1:]:
        c.start()
    for c in copies + [load]:
        c.wait()

    def store(k, part, kp, value):
        out[k, part, 128 * kp : 128 * kp + 128, :] = value

    image_pair(xbuf, 0, tab, hbuf, ybuf, store)


def rest_kernel(
    img, tables, sent_a, e0, e1, wrapped, sent_b, xbuf, tab, hbuf, ybuf, sems
):
    at = place()
    copies = image_copies(img, 1 - at["lo"], (2, 3), xbuf, sems)
    copies += image_copies(img, at["lo"], range(4), xbuf.at[pl.ds(2, 4)], sems.at[pl.ds(2, 4)])
    load = pltpu.make_async_copy(tables.at[pl.ds(0, 2)], tab, sems.at[6])
    for c in copies[:1] + [load] + copies[1:]:
        c.start()
    lo = at["lo"] > 0
    zero = at["zero"]
    load.wait()

    def keep(k, part, kp, value):
        sent_b[k, part, 128 * kp : 128 * kp + 128, :] = value

    for pair in range(3):
        for c in copies[2 * pair : 2 * pair + 2]:
            c.wait()

        def store(k, part, kp, value):
            rows = slice(128 * kp, 128 * kp + 128)
            sent = (sent_a, sent_b)[pair - 1]
            other = sent[k, part, rows, :]
            v0 = jnp.where(lo, other, value)
            v1 = jnp.where(lo, value, other)
            p = 2 * (pair - 1) + k
            e0[p, part, rows, :] = v0
            e1[p, part, rows, :] = v1
            wrapped[p, part, rows, :] = jnp.where(zero, v0, v1)

        image_pair(xbuf, 2 * pair, tab, hbuf.at[pair], ybuf.at[pair], store if pair else keep)


VM = pl.BlockSpec(memory_space=pltpu.VMEM)
SM = pl.BlockSpec(memory_space=pltpu.SMEM)
ANY = pl.BlockSpec(memory_space=pl.ANY)


def call(kernel, outs, ins, scratch, limit, flops, name):
    specs = []
    for kind, _ in ins:
        specs.append({"s": SM, "v": VM, "a": ANY}[kind])
    return pl.pallas_call(
        kernel,
        out_shape=[jax.ShapeDtypeStruct(s, t) for s, t in outs],
        in_specs=specs,
        out_specs=[VM] * len(outs),
        scratch_shapes=scratch,
        compiler_params=pltpu.CompilerParams(vmem_limit_bytes=limit * 2**20),
        cost_estimate=pl.CostEstimate(flops=flops * 10**6, bytes_accessed=2**20, transcendentals=0),
        name=name,
    )(*[a for _, a in ins])


def forward_send(patches, images, tables):
    return call(
        functools.partial(send_kernel, patches),
        [((2, 2, BAND, BAND), BF)],
        [("a", images), ("a", tables)],
        [
            pltpu.VMEM((2, 2, PIX, PIX), BF),
            pltpu.VMEM((2, 256, 512), BF),
            pltpu.VMEM((2, 1024, 512), BF),
            pltpu.VMEM((2, 512, 512), BF),
            pltpu.SemaphoreType.DMA((3,)),
        ],
        57,
        1200,
        "forward_send",
    )[0]


def forward_rest(images, tables, sent_a):
    return call(
        rest_kernel,
        [((4, 2, BAND, BAND), BF)] * 3 + [((2, 2, BAND, BAND), BF)],
        [("a", images), ("a", tables), ("v", sent_a)],
        [
            pltpu.VMEM((6, 2, PIX, PIX), BF),
            pltpu.VMEM((2, 256, 512), BF),
            pltpu.VMEM((3, 2, 1024, 512), BF),
            pltpu.VMEM((3, 2, 512, 512), BF),
            pltpu.SemaphoreType.DMA((7,)),
        ],
        REST_LIMIT,
        3600,
        "forward_rest",
    )


def load_block(ref, p, row, lane):
    return [ref[p, part, pl.ds(row, 16), lane].astype(F32) for part in range(2)]


def accumulate(acc, i, l, m):
    acc[2 * i] = acc[2 * i] + (l[0] * m[0] + l[1] * m[1])
    acc[2 * i + 1] = acc[2 * i + 1] + (l[1] * m[0] - l[0] * m[1])


def add_energy(energy, i, w, s):
    energy[i] = energy[i] + w * (s[0] * s[0] + s[1] * s[1])


def pick(cond, a, b):
    return [jnp.where(cond, u, v) for u, v in zip(a, b)]


def inverse(tab, cross, surf, pairs, at):
    for i in range(pairs):
        shifted = dot(tab[0], cross[i]).astype(BF)
        low = dot(tab[1], cross[i]).astype(BF)
        surf[at + i] = (dot_nt(shifted, tab[2, :, :BAND]) + dot_nt(low, tab[2, :, BAND:])).astype(BF)


def emit(surf, pairs, outs, erows):
    x = place()["x"]
    for slot, out in enumerate(outs):
        dest = lax.rem(x + slot, 4)
        for yh in range(2):
            start = pl.multiple_of((4 * yh + dest) * 32, 32)
            for i in range(pairs):
                out[yh, 32 * i : 32 * i + 32, :] = surf[i, pl.ds(start, 32), :]
            out[yh, 32 * pairs :, :] = erows


def split(value):
    hi = value.astype(BF).astype(F32)
    return hi, (value - hi).astype(BF).astype(F32)


def energy_rows(values):
    his, los = zip(*[split(v) for v in values])
    pad = [jnp.zeros_like(values[0])] * (EROWS - 2 * len(values))
    return jnp.concatenate(list(his) + list(los) + pad, axis=0).astype(BF)


def total_rows(energy_sum, count):
    totals = []
    for i in range(count):
        total = jnp.sum(jnp.sum(energy_sum[i], axis=1, keepdims=True), axis=0, keepdims=True)
        totals.append(jnp.broadcast_to(total, (1, WIN)))
    return energy_rows(totals)


def blocks(body):
    @pl.loop(0, BAND // 16)
    def _(block):
        row = pl.multiple_of(block * 16, 16)
        rowi = pl.multiple_of(block * 16 + BAND, 16)
        for half in range(2):
            body(row, rowi, slice(128 * half, 128 * half + 128))


def zeros(count):
    return [jnp.zeros((16, 128), F32)] * count


def early_kernel(weight, tab, e0, e1, q1, op_a, op_b, surf, energy_out, cross):
    lo = place()["lo"] > 0
    energy_out[...] = jnp.zeros_like(energy_out)

    def body(row, rowi, lane):
        acc, energy = zeros(8), zeros(4)
        for p in range(4):
            w = weight[p]
            own0, own1 = load_block(e0, p, row, lane), load_block(e1, p, row, lane)
            opp = load_block((op_a, op_b)[p // 2], p % 2, row, lane)
            prev = load_block(q1, p, row, lane)
            for i, v in enumerate((own0, own1, opp, prev)):
                add_energy(energy, i, w, v)
            accumulate(acc, 0, [w * v for v in own0], own1)
            accumulate(acc, 1, [w * v for v in pick(lo, own1, own0)], opp)
            wq = [w * v for v in prev]
            accumulate(acc, 2, wq, own0)
            accumulate(acc, 3, wq, own1)
        for i, at in enumerate((0, 1, 3, 4)):
            cross[at, pl.ds(row, 16), lane] = acc[2 * i].astype(BF)
            cross[at, pl.ds(rowi, 16), lane] = acc[2 * i + 1].astype(BF)
        cross[2, pl.ds(row, 16), lane] = acc[2].astype(BF)
        cross[2, pl.ds(rowi, 16), lane] = (-acc[3]).astype(BF)
        for i in range(4):
            energy_out[i] += energy[i][:8] + energy[i][8:]

    blocks(body)
    inverse(tab, cross, surf, 5, 0)


def late_kernel(
    weight, tab, early, energy_in, e0, q1, pl0, pl1, turn_a, turn_b, s0, s1, s2, s3, cross, surf, energy_sum
):
    at = place()
    swapped, end = at["last"], at["end"]
    energy_sum[0:4] = energy_in[...]
    energy_sum[4:6] = jnp.zeros((2, 8, 128), F32)

    def body(row, rowi, lane):
        acc, energy = zeros(6), zeros(2)
        for p in range(4):
            w = weight[p]
            own0 = load_block(e0, p, row, lane)
            prev = load_block(q1, p, row, lane)
            turned = (turn_a, turn_b)[p // 2]
            a = [
                jnp.where(end, turned[p % 2, part, pl.ds(row, 16), lane], pl0[p, part, pl.ds(row, 16), lane]).astype(F32)
                for part in range(2)
            ]
            b = load_block(pl1, p, row, lane)
            next0, next1 = pick(swapped, b, a), pick(swapped, a, b)
            for i, v in enumerate((next0, next1)):
                add_energy(energy, i, w, v)
            w0 = [w * v for v in own0]
            wq = [w * v for v in prev]
            for i, (l, m) in enumerate(
                ((w0, next0), (w0, next1), (wq, next0))
            ):
                accumulate(acc, i, l, m)
        for i in range(3):
            cross[i, pl.ds(row, 16), lane] = acc[2 * i].astype(BF)
            cross[i, pl.ds(rowi, 16), lane] = acc[2 * i + 1].astype(BF)
        for i in range(2):
            energy_sum[4 + i] += energy[i][:8] + energy[i][8:]

    blocks(body)
    surf[0:5] = early[...]
    inverse(tab, cross, surf, 3, 5)
    emit(surf, 8, (s0, s1, s2, s3), total_rows(energy_sum, 6))


def surfaces(kernel, pairs, outs, ins, scratch, name):
    return call(
        kernel,
        outs,
        ins,
        [pltpu.VMEM((pairs, 2 * BAND, BAND), BF)] + scratch,
        28,
        250 * pairs,
        name,
    )


def sum_energy(block, count):
    return [block[i : i + 1] + block[count + i : count + i + 1] for i in range(count)]


def add_parts(parts, h):
    a, b, c, d = [r[h].astype(F32) for r in parts]
    return (a + b) + (c + d)


def gather_kernel(a, b, c, d, keep, near, back_same, back_other, opp_same, opp_other):
    yh = place()["yh"]
    for h, (near_out, back_out, opp_out) in (
        (yh, (keep, back_same, opp_same)),
        (1 - yh, (near, back_other, opp_other)),
    ):
        total = add_parts((a, b, c, d), h)
        erows = energy_rows(sum_energy(total[256:], 6))
        near_out[0:64] = total[0:64].astype(near_out.dtype)
        near_out[64:128] = total[160:224].astype(near_out.dtype)
        near_out[128:] = erows.astype(near_out.dtype)
        back_out[0:64] = total[96:160].astype(BF)
        back_out[64:96] = total[224:256].astype(BF)
        back_out[96:] = erows
        opp_out[0:32] = total[64:96].astype(BF)
        opp_out[32:] = erows


def final_kernel(scale, mask, keep, near, back_a, back_b, opp_a, opp_b, out):
    lo = place()["lo"] > 0
    mine = keep[...] + near[...].astype(F32)
    back = back_a[...].astype(F32) + back_b[...].astype(F32)
    other = opp_a[...].astype(F32) + opp_b[...].astype(F32)

    def factor(el, em):
        return scale / jnp.sqrt(el * em)

    def put(look, lag, value):
        out[look, lag] = value * mask[look, lag].astype(F32)

    own0, own1, opp, _, next0, next1 = sum_energy(mine[128:], 6)
    put(0, 0, mine[:32] * factor(own0, own1))
    put(0, 1, mine[64:96] * factor(own0, next0))
    put(0, 2, mine[96:128] * factor(own0, next1))
    b0, b1, _, bq, bn0, _ = sum_energy(back[96:], 6)
    put(1, 0, back[:32] * factor(bq, b0))
    put(1, 1, back[32:64] * factor(bq, b1))
    put(1, 2, back[64:96] * factor(bq, bn0))
    o0, o1, oo, _, _, _ = sum_energy(other[32:], 6)
    own_opp = mine[32:64] * factor(jnp.where(lo, own1, own0), opp)
    other_opp = other[:32] * factor(jnp.where(lo, o0, o1), oo)
    put(0, 3, jnp.where(lo, other_opp, own_opp))
    put(1, 3, jnp.where(lo, own_opp, other_opp))


def after(array, *others):
    return lax.optimization_barrier((array,) + others)[0]


def per_device(images, patch_weight, pair_mask):
    nlook = lax.axis_size("look")
    nswath = lax.axis_size("swath")
    ring = nlook // 2
    tables, inverse_tables = make_tables()

    def over_look(array, to):
        return lax.ppermute(array, "look", [(i, to(i)) for i in range(nlook)])

    def over_x(parts):
        moved = [parts[0]]
        for by in range(1, 4):
            perm = [(i, i // 4 * 4 + (i + by) % 4) for i in range(nswath)]
            moved.append(lax.ppermute(parts[by], "swath", perm))
        return moved

    def over_both(array, to_look, flip):
        perm = [
            (i * nswath + s, to_look(i) * nswath + ((s + nswath // 2) % nswath if flip else s))
            for i in range(nlook)
            for s in range(nswath)
        ]
        return lax.ppermute(array, ("look", "swath"), perm)

    stay = lambda i: i
    ahead = lambda i: (i + 1) % nlook
    behind = lambda i: (i - 1) % nlook
    across = lambda i: (i + ring) % nlook
    turn = lambda i: i // ring * ring + (i - 1) % ring

    sent_a = forward_send((0, 1), images, tables)
    op_a = over_look(sent_a, across)
    e0, e1, wrapped, sent_b = forward_rest(images, tables, sent_a)
    op_b = over_look(sent_b, across)
    pl0 = lax.ppermute(e0, "look", [(i, turn(i)) for i in range(nlook) if i % ring])
    edges = [(i, turn(i)) for i in range(nlook) if i % ring == 0]
    turn_a = lax.ppermute(op_a, "look", edges)
    op_b = after(op_b, pl0, turn_a)
    turn_b = lax.ppermute(op_b, "look", edges)
    pl1 = over_look(after(wrapped, op_b), behind)
    q1 = over_look(after(e1, op_b), ahead)

    vm = lambda *arrays: [("v", a) for a in arrays]
    common = [("s", patch_weight), ("v", inverse_tables)]
    surf, energy = surfaces(
        early_kernel,
        5,
        [((5, WIN, WIN), BF), ((4, 8, 128), F32)],
        common + vm(e0, e1, q1, op_a, op_b),
        [],
        "surfaces_early",
    )
    parts = surfaces(
        late_kernel,
        3,
        [((2, 8 * 32 + EROWS, WIN), BF)] * 4,
        common + vm(surf, energy, e0, q1, pl0, pl1, turn_a, turn_b),
        [pltpu.VMEM((8, WIN, WIN), BF), pltpu.VMEM((6, 8, 128), F32)],
        "surfaces_late",
    )
    rows = lambda n, t: ((n + EROWS, WIN), t)
    keep, near, back_same, back_other, opp_same, opp_other = call(
        gather_kernel,
        [rows(128, F32), rows(128, BF), rows(96, BF), rows(96, BF), rows(32, BF), rows(32, BF)],
        vm(*over_x(parts)),
        [],
        16,
        10,
        "gather",
    )
    got = (
        keep,
        over_both(near, stay, True),
        over_both(back_same, behind, False),
        over_both(back_other, behind, True),
        over_both(opp_same, across, False),
        over_both(opp_other, across, True),
    )
    scale = BAND * math.sqrt(patch_weight.shape[0] * nswath)
    return call(
        functools.partial(final_kernel, scale),
        [((2, 4, 32, WIN), F32)],
        [("s", pair_mask)] + vm(*got),
        [],
        16,
        10,
        "final",
    )[0]


def solution(mesh):
    return jax.shard_map(
        per_device,
        mesh=mesh,
        in_specs=(P("look", "swath", None, None, None), P("swath"), P("look", None)),
        out_specs=P("look", None, "swath", None),
        check_vma=False,
    )
```

```python
import functools
import math

import jax
import jax.numpy as jnp
import numpy as np
from jax import lax
from jax.experimental import pallas as pl
from jax.experimental.pallas import tpu as pltpu
from jax.sharding import PartitionSpec as P

PIX = 512
BAND = 256
WIN = 256
HALF = 256
CHUNK = 2
EROWS = 16
TABLES = 32
REST_LIMIT = 46
BF = jnp.bfloat16
F32 = jnp.float32


def phases(rows, cols):
    phase = (rows[:, None] * cols[None, :]) % PIX
    angle = (2.0 * math.pi / PIX * phase.astype(np.float32)).astype(np.float32)
    return np.cos(angle), np.sin(angle)


def make_tables():
    order = np.concatenate([np.arange(0, BAND, 2), np.arange(1, BAND, 2)])
    n0 = np.arange(HALF)
    left = []
    for parity in range(2):
        ks = np.arange(parity, BAND, 2) - BAND // 2
        re, im = phases(ks, n0)
        im = -im
        left.append(np.block([[re, -im], [im, re]]))
    ts = np.arange(WIN) - WIN // 2
    gre, gim = phases(ts, order - BAND // 2)
    first = np.block([[gre, -gim], [gim, gre]])
    second = np.concatenate([gre, -gim], axis=1)
    cast = lambda a: jnp.asarray(np.asarray(a, np.float32).astype(jnp.bfloat16))
    room = np.zeros((TABLES - 2, 256, 512))
    return cast(np.concatenate([np.stack(left), room])), cast(np.stack([first[:256], first[256:], second]))


def place():
    look = lax.axis_index("look")
    swath = lax.axis_index("swath")
    nlook = lax.axis_size("look")
    return dict(
        lo=(look >= nlook // 2).astype(jnp.int32),
        zero=look == 0,
        last=look == nlook - 1,
        end=lax.rem(look, nlook // 2) == nlook // 2 - 1,
        x=lax.rem(swath, 4),
        yh=swath // 4,
    )


def dot(a, b):
    return jnp.dot(a, b, preferred_element_type=F32)


def dot_nt(a, b):
    return lax.dot_general(a, b, (((1,), (1,)), ((), ())), preferred_element_type=F32)


def butterflies(x):
    x00 = x[:HALF, :HALF].astype(F32)
    x01 = x[:HALF, HALF:].astype(F32)
    x10 = x[HALF:, :HALF].astype(F32)
    x11 = x[HALF:, HALF:].astype(F32)
    a, b = x00 + x10, x01 + x11
    c, d = x00 - x10, x01 - x11
    return [v.astype(BF) for v in (a + b, a - b, c + d, c - d)]


def image_pair(xbuf, at, tab, hbuf, ybuf, store):
    for k in range(2):
        for part in range(2):
            for q, h in enumerate(butterflies(xbuf.at[at + k, part])):
                kp, lp = q // 2, q % 2
                row = 512 * k + 256 * kp
                hbuf[lp, row : row + 256, 256 * part : 256 * part + 256] = h
    for lp in range(2):
        y = dot_nt(hbuf[lp], tab[lp]).astype(BF)
        for k in range(2):
            for kp in range(2):
                block = y[512 * k + 256 * kp : 512 * k + 256 * kp + 256]
                lane = 256 * k + 128 * lp
                ybuf[kp, :256, lane : lane + 128] = block[:, :128]
                ybuf[kp, 256:, lane : lane + 128] = block[:, 128:]
    for kp in range(2):
        spec = dot(tab[kp], ybuf[kp]).astype(BF)
        for k in range(2):
            for part in range(2):
                store(k, part, kp, spec[128 * part : 128 * part + 128, 256 * k : 256 * k + 256])


def image_copies(img, look, patches, xbuf, sems):
    return [
        pltpu.make_async_copy(img.at[look, p], xbuf.at[i], sems.at[i]) for i, p in enumerate(patches)
    ]


def send_kernel(patches, img, tables, out, xbuf, tab, hbuf, ybuf, sems):
    copies = image_copies(img, 1 - place()["lo"], patches, xbuf, sems)
    load = pltpu.make_async_copy(tables.at[pl.ds(0, 2)], tab, sems.at[len(patches)])
    for c in copies[:1] + [load] + copies[1:]:
        c.start()
    for c in copies + [load]:
        c.wait()

    def store(k, part, kp, value):
        out[k, part, 128 * kp : 128 * kp + 128, :] = value

    image_pair(xbuf, 0, tab, hbuf, ybuf, store)


def rest_kernel(
    img, tables, sent_a, e0, e1, wrapped, sent_b, xbuf, tab, hbuf, ybuf, sems
):
    at = place()
    copies = image_copies(img, 1 - at["lo"], (2, 3), xbuf, sems)
    copies += image_copies(img, at["lo"], range(4), xbuf.at[pl.ds(2, 4)], sems.at[pl.ds(2, 4)])
    load = pltpu.make_async_copy(tables.at[pl.ds(0, 2)], tab, sems.at[6])
    for c in copies[:1] + [load] + copies[1:]:
        c.start()
    lo = at["lo"] > 0
    zero = at["zero"]
    load.wait()

    def keep(k, part, kp, value):
        sent_b[k, part, 128 * kp : 128 * kp + 128, :] = value

    for pair in range(3):
        for c in copies[2 * pair : 2 * pair + 2]:
            c.wait()

        def store(k, part, kp, value):
            rows = slice(128 * kp, 128 * kp + 128)
            sent = (sent_a, sent_b)[pair - 1]
            other = sent[k, part, rows, :]
            v0 = jnp.where(lo, other, value)
            v1 = jnp.where(lo, value, other)
            p = 2 * (pair - 1) + k
            e0[p, part, rows, :] = v0
            e1[p, part, rows, :] = v1
            wrapped[p, part, rows, :] = jnp.where(zero, v0, v1)

        image_pair(xbuf, 2 * pair, tab, hbuf.at[pair], ybuf.at[pair], store if pair else keep)


VM = pl.BlockSpec(memory_space=pltpu.VMEM)
SM = pl.BlockSpec(memory_space=pltpu.SMEM)
ANY = pl.BlockSpec(memory_space=pl.ANY)


def call(kernel, outs, ins, scratch, limit, flops, name):
    specs = []
    for kind, _ in ins:
        specs.append({"s": SM, "v": VM, "a": ANY}[kind])
    return pl.pallas_call(
        kernel,
        out_shape=[jax.ShapeDtypeStruct(s, t) for s, t in outs],
        in_specs=specs,
        out_specs=[VM] * len(outs),
        scratch_shapes=scratch,
        compiler_params=pltpu.CompilerParams(vmem_limit_bytes=limit * 2**20),
        cost_estimate=pl.CostEstimate(flops=flops * 10**6, bytes_accessed=2**20, transcendentals=0),
        name=name,
    )(*[a for _, a in ins])


def forward_send(patches, images, tables):
    return call(
        functools.partial(send_kernel, patches),
        [((2, 2, BAND, BAND), BF)],
        [("a", images), ("a", tables)],
        [
            pltpu.VMEM((2, 2, PIX, PIX), BF),
            pltpu.VMEM((2, 256, 512), BF),
            pltpu.VMEM((2, 1024, 512), BF),
            pltpu.VMEM((2, 512, 512), BF),
            pltpu.SemaphoreType.DMA((3,)),
        ],
        57,
        1200,
        "forward_send",
    )[0]


def forward_rest(images, tables, sent_a):
    return call(
        rest_kernel,
        [((4, 2, BAND, BAND), BF)] * 3 + [((2, 2, BAND, BAND), BF)],
        [("a", images), ("a", tables), ("v", sent_a)],
        [
            pltpu.VMEM((6, 2, PIX, PIX), BF),
            pltpu.VMEM((2, 256, 512), BF),
            pltpu.VMEM((3, 2, 1024, 512), BF),
            pltpu.VMEM((3, 2, 512, 512), BF),
            pltpu.SemaphoreType.DMA((7,)),
        ],
        REST_LIMIT,
        3600,
        "forward_rest",
    )


def load_block(ref, p, row, lane):
    return [ref[p, part, pl.ds(row, 16), lane].astype(F32) for part in range(2)]


def accumulate(acc, i, l, m):
    acc[2 * i] = acc[2 * i] + (l[0] * m[0] + l[1] * m[1])
    acc[2 * i + 1] = acc[2 * i + 1] + (l[1] * m[0] - l[0] * m[1])


def add_energy(energy, i, w, s):
    energy[i] = energy[i] + w * (s[0] * s[0] + s[1] * s[1])


def pick(cond, a, b):
    return [jnp.where(cond, u, v) for u, v in zip(a, b)]


def inverse(tab, cross, surf, pairs, at):
    for i in range(pairs):
        shifted = dot(tab[0], cross[i]).astype(BF)
        low = dot(tab[1], cross[i]).astype(BF)
        surf[at + i] = (dot_nt(shifted, tab[2, :, :BAND]) + dot_nt(low, tab[2, :, BAND:])).astype(BF)


def emit(surf, pairs, outs, erows):
    x = place()["x"]
    for slot, out in enumerate(outs):
        dest = lax.rem(x + slot, 4)
        for yh in range(2):
            start = pl.multiple_of((4 * yh + dest) * 32, 32)
            for i in range(pairs):
                out[yh, 32 * i : 32 * i + 32, :] = surf[i, pl.ds(start, 32), :]
            out[yh, 32 * pairs :, :] = erows


def split(value):
    hi = value.astype(BF).astype(F32)
    return hi, (value - hi).astype(BF).astype(F32)


def energy_rows(values):
    his, los = zip(*[split(v) for v in values])
    pad = [jnp.zeros_like(values[0])] * (EROWS - 2 * len(values))
    return jnp.concatenate(list(his) + list(los) + pad, axis=0).astype(BF)


def total_rows(energy_sum, count):
    totals = []
    for i in range(count):
        total = jnp.sum(jnp.sum(energy_sum[i], axis=1, keepdims=True), axis=0, keepdims=True)
        totals.append(jnp.broadcast_to(total, (1, WIN)))
    return energy_rows(totals)


def blocks(body):
    @pl.loop(0, BAND // 16)
    def _(block):
        row = pl.multiple_of(block * 16, 16)
        rowi = pl.multiple_of(block * 16 + BAND, 16)
        for half in range(2):
            body(row, rowi, slice(128 * half, 128 * half + 128))


def zeros(count):
    return [jnp.zeros((16, 128), F32)] * count


def early_kernel(weight, tab, e0, e1, op_a, op_b, surf, energy_out, cross):
    lo = place()["lo"] > 0
    energy_out[...] = jnp.zeros_like(energy_out)

    def body(row, rowi, lane):
        acc, energy = zeros(4), zeros(3)
        for p in range(4):
            w = weight[p]
            own0, own1 = load_block(e0, p, row, lane), load_block(e1, p, row, lane)
            opp = load_block((op_a, op_b)[p // 2], p % 2, row, lane)
            for i, v in enumerate((own0, own1, opp)):
                add_energy(energy, i, w, v)
            accumulate(acc, 0, [w * v for v in own0], own1)
            accumulate(acc, 1, [w * v for v in pick(lo, own1, own0)], opp)
        for i in range(2):
            cross[i, pl.ds(row, 16), lane] = acc[2 * i].astype(BF)
            cross[i, pl.ds(rowi, 16), lane] = acc[2 * i + 1].astype(BF)
        cross[2, pl.ds(row, 16), lane] = acc[2].astype(BF)
        cross[2, pl.ds(rowi, 16), lane] = (-acc[3]).astype(BF)
        for i in range(3):
            energy_out[i] += energy[i][:8] + energy[i][8:]

    blocks(body)
    inverse(tab, cross, surf, 3, 0)


def late_kernel(
    weight, tab, early, energy_in, e0, e1, q1, pl0, pl1, turn_a, turn_b, s0, s1, s2, s3, cross, surf, energy_sum
):
    at = place()
    swapped, end = at["last"], at["end"]
    energy_sum[0:3] = energy_in[...]
    energy_sum[3:6] = jnp.zeros((3, 8, 128), F32)

    def body(row, rowi, lane):
        acc, energy = zeros(10), zeros(3)
        for p in range(4):
            w = weight[p]
            own0, own1 = load_block(e0, p, row, lane), load_block(e1, p, row, lane)
            prev = load_block(q1, p, row, lane)
            turned = (turn_a, turn_b)[p // 2]
            a = [
                jnp.where(end, turned[p % 2, part, pl.ds(row, 16), lane], pl0[p, part, pl.ds(row, 16), lane]).astype(F32)
                for part in range(2)
            ]
            b = load_block(pl1, p, row, lane)
            next0, next1 = pick(swapped, b, a), pick(swapped, a, b)
            for i, v in enumerate((prev, next0, next1)):
                add_energy(energy, i, w, v)
            w0 = [w * v for v in own0]
            wq = [w * v for v in prev]
            for i, (l, m) in enumerate(
                ((w0, next0), (w0, next1), (wq, own0), (wq, own1), (wq, next0))
            ):
                accumulate(acc, i, l, m)
        for i in range(5):
            cross[i, pl.ds(row, 16), lane] = acc[2 * i].astype(BF)
            cross[i, pl.ds(rowi, 16), lane] = acc[2 * i + 1].astype(BF)
        for i in range(3):
            energy_sum[3 + i] += energy[i][:8] + energy[i][8:]

    blocks(body)
    surf[0:3] = early[...]
    inverse(tab, cross, surf, 5, 3)
    emit(surf, 8, (s0, s1, s2, s3), total_rows(energy_sum, 6))


def surfaces(kernel, pairs, outs, ins, scratch, name):
    return call(
        kernel,
        outs,
        ins,
        [pltpu.VMEM((pairs, 2 * BAND, BAND), BF)] + scratch,
        28,
        250 * pairs,
        name,
    )


def sum_energy(block, count):
    return [block[i : i + 1] + block[count + i : count + i + 1] for i in range(count)]


def add_parts(parts, h):
    a, b, c, d = [r[h].astype(F32) for r in parts]
    return (a + b) + (c + d)


def gather_kernel(a, b, c, d, keep, near, back_same, back_other, opp_same, opp_other):
    yh = place()["yh"]
    for h, (near_out, back_out, opp_out) in (
        (yh, (keep, back_same, opp_same)),
        (1 - yh, (near, back_other, opp_other)),
    ):
        total = add_parts((a, b, c, d), h)
        erows = energy_rows(sum_energy(total[256:], 6))
        near_out[0:64] = total[0:64].astype(near_out.dtype)
        near_out[64:128] = total[96:160].astype(near_out.dtype)
        near_out[128:] = erows.astype(near_out.dtype)
        back_out[0:96] = total[160:256].astype(BF)
        back_out[96:] = erows
        opp_out[0:32] = total[64:96].astype(BF)
        opp_out[32:] = erows


def final_kernel(scale, mask, keep, near, back_a, back_b, opp_a, opp_b, out):
    lo = place()["lo"] > 0
    mine = keep[...] + near[...].astype(F32)
    back = back_a[...].astype(F32) + back_b[...].astype(F32)
    other = opp_a[...].astype(F32) + opp_b[...].astype(F32)

    def factor(el, em):
        return scale / jnp.sqrt(el * em)

    def put(look, lag, value):
        out[look, lag] = value * mask[look, lag].astype(F32)

    own0, own1, opp, _, next0, next1 = sum_energy(mine[128:], 6)
    put(0, 0, mine[:32] * factor(own0, own1))
    put(0, 1, mine[64:96] * factor(own0, next0))
    put(0, 2, mine[96:128] * factor(own0, next1))
    b0, b1, _, bq, bn0, _ = sum_energy(back[96:], 6)
    put(1, 0, back[:32] * factor(bq, b0))
    put(1, 1, back[32:64] * factor(bq, b1))
    put(1, 2, back[64:96] * factor(bq, bn0))
    o0, o1, oo, _, _, _ = sum_energy(other[32:], 6)
    own_opp = mine[32:64] * factor(jnp.where(lo, own1, own0), opp)
    other_opp = other[:32] * factor(jnp.where(lo, o0, o1), oo)
    put(0, 3, jnp.where(lo, other_opp, own_opp))
    put(1, 3, jnp.where(lo, own_opp, other_opp))


def after(array, *others):
    return lax.optimization_barrier((array,) + others)[0]


def per_device(images, patch_weight, pair_mask):
    nlook = lax.axis_size("look")
    nswath = lax.axis_size("swath")
    ring = nlook // 2
    tables, inverse_tables = make_tables()

    def over_look(array, to):
        return lax.ppermute(array, "look", [(i, to(i)) for i in range(nlook)])

    def over_x(parts):
        moved = [parts[0]]
        for by in range(1, 4):
            perm = [(i, i // 4 * 4 + (i + by) % 4) for i in range(nswath)]
            moved.append(lax.ppermute(parts[by], "swath", perm))
        return moved

    def over_both(array, to_look, flip):
        perm = [
            (i * nswath + s, to_look(i) * nswath + ((s + nswath // 2) % nswath if flip else s))
            for i in range(nlook)
            for s in range(nswath)
        ]
        return lax.ppermute(array, ("look", "swath"), perm)

    stay = lambda i: i
    ahead = lambda i: (i + 1) % nlook
    behind = lambda i: (i - 1) % nlook
    across = lambda i: (i + ring) % nlook
    turn = lambda i: i // ring * ring + (i - 1) % ring

    sent_a = forward_send((0, 1), images, tables)
    op_a = over_look(sent_a, across)
    e0, e1, wrapped, sent_b = forward_rest(images, tables, sent_a)
    op_b = over_look(sent_b, across)
    pl0 = lax.ppermute(e0, "look", [(i, turn(i)) for i in range(nlook) if i % ring])
    edges = [(i, turn(i)) for i in range(nlook) if i % ring == 0]
    turn_a = lax.ppermute(op_a, "look", edges)
    op_b = after(op_b, pl0, turn_a)
    turn_b = lax.ppermute(op_b, "look", edges)
    pl1 = over_look(after(wrapped, op_b), behind)
    q1 = over_look(after(e1, op_b), ahead)

    vm = lambda *arrays: [("v", a) for a in arrays]
    common = [("s", patch_weight), ("v", inverse_tables)]
    surf, energy = surfaces(
        early_kernel,
        3,
        [((3, WIN, WIN), BF), ((3, 8, 128), F32)],
        common + vm(e0, e1, op_a, op_b),
        [],
        "surfaces_early",
    )
    parts = surfaces(
        late_kernel,
        5,
        [((2, 8 * 32 + EROWS, WIN), BF)] * 4,
        common + vm(surf, energy, e0, e1, q1, pl0, pl1, turn_a, turn_b),
        [pltpu.VMEM((8, WIN, WIN), BF), pltpu.VMEM((6, 8, 128), F32)],
        "surfaces_late",
    )
    rows = lambda n, t: ((n + EROWS, WIN), t)
    keep, near, back_same, back_other, opp_same, opp_other = call(
        gather_kernel,
        [rows(128, F32), rows(128, BF), rows(96, BF), rows(96, BF), rows(32, BF), rows(32, BF)],
        vm(*over_x(parts)),
        [],
        16,
        10,
        "gather",
    )
    got = (
        keep,
        over_both(near, stay, True),
        over_both(back_same, behind, False),
        over_both(back_other, behind, True),
        over_both(opp_same, across, False),
        over_both(opp_other, across, True),
    )
    scale = BAND * math.sqrt(patch_weight.shape[0] * nswath)
    return call(
        functools.partial(final_kernel, scale),
        [((2, 4, 32, WIN), F32)],
        [("s", pair_mask)] + vm(*got),
        [],
        16,
        10,
        "final",
    )[0]


def solution(mesh):
    return jax.shard_map(
        per_device,
        mesh=mesh,
        in_specs=(P("look", "swath", None, None, None), P("swath"), P("look", None)),
        out_specs=P("look", None, "swath", None),
        check_vma=False,
    )
```
